32 devices in a mesh: tm: 32 (over z, y, x, core), rows: 1.
Axes of the slice: x: 2, y: 2, z: 4, core: 2. Of those that a mesh axis runs over, the one named last changes fastest.
Arguments:
- latent: bfloat16 [32, 2, 128, 512], P('tm', 'rows'), may hold values from -32 to 32
- norm_gain: float32 [512], replicated, may hold values from 0.1 to 1.9
- conv_weight: bfloat16 [27, 512, 512], P(None, 'tm'), may hold values from -0.0546875 to 0.0546875
- grad_out: bfloat16 [32, 2, 128, 512], P('tm', 'rows'), may hold values from -6 to 6
Outputs:
- refined: bfloat16 [32, 2, 128, 512], P('tm', 'rows')
- grad_latent: float32 [32, 2, 128, 512], P('tm', 'rows')
The draws below stay inside these ranges and needn't reach their ends.
All inputs are finite; a program needn't handle non-finite values.
Results may differ from the reference program's by a relative error of at most 0.0013.
The reference program's roundings to bfloat16 on the way (of `activated`) count: a program that leaves them out, or rounds other values in their place, can miss the bound.
Values may be sent and summed in bfloat16 or wider, within the bound.
A program may use at most 64 MiB of HBM per device.

```python
import jax
import jax.numpy as jnp
from jax import lax

C = 512
GROUPS = 32
TAPS = 27
COLS = 128
FRAMES = 32
HEIGHT = 2


def draw_latent(key, part):
    key_mean, key_rough, key_noise = jax.random.split(key, 3)
    positions = jnp.arange(HEIGHT, dtype=jnp.float32) / max(HEIGHT - 1, 1)
    channel_mean = jnp.clip(jax.random.normal(key_mean, (C,), jnp.float32), -4.0, 4.0)
    rough = jnp.exp(jax.random.uniform(key_rough, (FRAMES, HEIGHT, COLS, 1), jnp.float32, -0.7, 0.7))
    rise = 1.0 + 2.0 * positions
    noise = jnp.clip(jax.random.normal(key_noise, (FRAMES, HEIGHT, COLS, C), jnp.float32), -4.0, 4.0)
    values = rise[None, :, None, None] * (0.5 * channel_mean + noise * rough)
    return jnp.clip(values, -32.0, 32.0).astype(jnp.bfloat16)


def level_of(rng, extent, cuts, low, top_value):
    factor_of, own = 1.0, jax.random.fold_in(rng, 6)
    for position, blocks in cuts:
        draws = jnp.exp(jax.random.uniform(jax.random.fold_in(own, position), (blocks,), jnp.float32, low / len(cuts), top_value / len(cuts)))
        factor_of = factor_of * jnp.repeat(draws, extent[position] // blocks).reshape([-1 if axis == position else 1 for axis in range(len(extent))])
    return factor_of


def normal_values(key, dims, deviation, most, shards=(), kind=jnp.bfloat16):
    entries = jax.random.normal(key, dims, jnp.float32) * deviation
    if len(shards) > 0:
        entries = level_of(key, dims, shards, -0.22, 0.18) * entries
    return jnp.clip(entries, min=-most, max=most).astype(kind)


def setup_inputs(seed: int = 0) -> dict:
    key_list = jax.random.split(jax.random.key(seed), 5)
    latent = draw_latent(jax.random.fold_in(key_list[4], 71), 0)
    norm_gain = jnp.clip(1.0 + 0.18 * jax.random.normal(key_list[1], (C,), jnp.float32), 0.1, 1.9)
    conv_weight = normal_values(key_list[2], (TAPS, C, C), (TAPS * C) ** -0.5, 0.0546875, ((1, 32),))
    grad_out = normal_values(key_list[3], (FRAMES, HEIGHT, COLS, C), 1.0, 6.0, ((0, 32),))
    return dict(latent=latent, norm_gain=norm_gain, conv_weight=conv_weight, grad_out=grad_out)


epsilon = 1e-06

def grouped_view(values):
    return values.reshape(values.shape[0], values.shape[1] * values.shape[2], GROUPS, values.shape[3] // GROUPS)

def reference(latent, norm_gain, conv_weight, grad_out):
    frames_all, height_all, columns, channels = latent.shape
    cell_count = height_all * columns * (channels // GROUPS)
    latent_wide = latent.astype(jnp.float32)
    grouped = grouped_view(latent_wide)
    average = lax.optimization_barrier(jnp.sum(grouped, axis=(1, 3))) / cell_count
    centred = grouped - average[:, None, :, None]
    spread = lax.optimization_barrier(jnp.sum(centred * centred, axis=(1, 3))) / cell_count
    inverse = lax.rsqrt(spread + epsilon)
    normed_grouped = centred * inverse[:, None, :, None]
    normed = normed_grouped.reshape(latent.shape)
    gain_wide = norm_gain.astype(jnp.float32)
    scaled = normed * gain_wide
    sigmoid_value = jax.nn.sigmoid(scaled)
    activated = (scaled * sigmoid_value).astype(jnp.bfloat16)
    weight_wide = conv_weight.astype(jnp.float32)
    padded = jnp.pad(activated, ((2, 0), (1, 1), (1, 1), (0, 0)))
    conv_sum = jnp.zeros((frames_all * height_all * columns, channels), jnp.float32)
    for time_tap in range(3):
        for row_tap in range(3):
            for col_tap in range(3):
                window = padded[time_tap:time_tap + frames_all, row_tap:row_tap + height_all, col_tap:col_tap + columns]
                conv_sum = conv_sum + jnp.dot(window.reshape(-1, channels).astype(jnp.float32), weight_wide[time_tap * 9 + row_tap * 3 + col_tap], preferred_element_type=jnp.float32)
    refined = (latent_wide + conv_sum.reshape(latent.shape)).astype(jnp.bfloat16)
    padded_grad = jnp.pad(grad_out, ((0, 2), (1, 1), (1, 1), (0, 0)))
    grad_act = jnp.zeros((frames_all * height_all * columns, channels), jnp.float32)
    for time_tap in range(3):
        for row_tap in range(3):
            for col_tap in range(3):
                window = padded_grad[2 - time_tap:2 - time_tap + frames_all, 2 - row_tap:2 - row_tap + height_all, 2 - col_tap:2 - col_tap + columns]
                grad_act = grad_act + jnp.dot(window.reshape(-1, channels).astype(jnp.float32), weight_wide[time_tap * 9 + row_tap * 3 + col_tap].T, preferred_element_type=jnp.float32)
    grad_scaled = grad_act.reshape(latent.shape) * sigmoid_value * (1.0 + scaled * (1.0 - sigmoid_value))
    grad_normed = grouped_view(grad_scaled * gain_wide)
    first = lax.optimization_barrier(jnp.sum(grad_normed, axis=(1, 3))) / cell_count
    second = lax.optimization_barrier(jnp.sum(grad_normed * normed_grouped, axis=(1, 3))) / cell_count
    grad_norm_part = (grad_normed - first[:, None, :, None] - normed_grouped * second[:, None, :, None]) * inverse[:, None, :, None]
    grad_latent = grad_out.astype(jnp.float32) + grad_norm_part.reshape(latent.shape)
    return (refined, grad_latent)
```

```python
import functools

import jax
import jax.numpy as jnp
from jax import lax
from jax.experimental import pallas as pl
from jax.experimental.pallas import tpu as pltpu
from jax.sharding import PartitionSpec as P

GROUPS = 32


epsilon = 1e-06


def shifted(block, axis, distance):
    devices = range(lax.axis_size(axis))
    route = [(i - distance, i) for i in devices if i - distance in devices]
    return lax.ppermute(block, axis, route)


def with_halo(shard, sides, width):
    for axis, dim in sides:
        size, length = (lax.axis_size(axis), shard.shape[dim])
        up = [(i, (i + 1) % size) for i in range(size - 1)]
        down = [(j, i) for i, j in up]
        last = lax.slice_in_dim(shard, length - width, length, axis=dim)
        first = lax.slice_in_dim(shard, 0, width, axis=dim)
        before = lax.ppermute(last, axis, up)
        after = lax.ppermute(first, axis, down)
        shard = jnp.concatenate([before, shard, after], axis=dim)
    return shard


def grouped_view(values):
    return values.reshape(
        values.shape[0], values.shape[1] * values.shape[2], GROUPS, values.shape[3] // GROUPS
    )


def widen_columns(values):
    return jnp.pad(values, ((0, 0), (0, 0), (1, 1), (0, 0)))


def group_mean(row, group, cells):
    channels = row.shape[1]
    shift = group.bit_length() - 1
    shape = (channels, channels)
    left = lax.shift_right_logical(lax.broadcasted_iota(jnp.int32, shape, 0), shift)
    right = lax.shift_right_logical(lax.broadcasted_iota(jnp.int32, shape, 1), shift)
    same = jnp.where(left == right, 1.0, 0.0).astype(jnp.float32)
    wide = jnp.broadcast_to(row, (8, channels))
    sums = jnp.dot(
        wide, same, preferred_element_type=jnp.float32, precision=lax.Precision.HIGHEST
    )
    return sums[0:1] / cells


def sums_of(values):
    return jnp.sum(values, axis=0, keepdims=True)


def block_kernel(
    n,
    columns,
    latent_ref,
    gain_ref,
    weight_ref,
    grad_ref,
    refined_ref,
    out_ref,
    whole,
    act_halo,
    grad_halo,
    act_wide,
    grad_wide,
    normed_ref,
    inverse_ref,
    conv_acc,
    grad_acc,
    own_sem,
    send_sem,
    recv_sem,
    halo_send,
    halo_recv,
):
    me = lax.axis_index("tm")
    depth = n // 8
    core = lax.rem(me, 2)
    px = lax.rem(lax.div(me, 2), 2)
    py = lax.rem(lax.div(me, 4), 2)
    pz = lax.div(me, 8)
    cells, channels = latent_ref.shape
    taps = weight_ref.shape[0]
    group = channels // GROUPS
    neighbour = {
        "x": me + 2 - 4 * px,
        "y": me + 4 - 8 * py,
        "core": me + 1 - 2 * core,
        "up": me + 8,
        "down": me - 8,
    }

    own_copy = pltpu.make_async_copy(weight_ref, whole.at[:, pz, py, px, core], own_sem)
    own_copy.start()

    barrier = pltpu.get_barrier_semaphore()

    def greet(other):
        pl.semaphore_signal(
            barrier, inc=1, device_id={"tm": other}, device_id_type=pl.DeviceIdType.MESH
        )

    for name in ("x", "y", "core"):
        greet(neighbour[name])
    linked = [
        (pz < depth - 1, me + 8),
        (pz > 0, me - 8),
        (me < n - 1, me + 1),
        (me < n - 2, me + 2),
        (me > 0, me - 1),
        (me > 1, me - 2),
    ]
    expected = jnp.int32(3)
    for there, other in linked:
        pl.when(there)(functools.partial(greet, other))
        expected = expected + there.astype(jnp.int32)
    own_copy.wait()
    pl.semaphore_wait(barrier, expected)

    n_last_z = taps // 5
    n_b = (taps - n_last_z) // 2
    n_c = taps - n_last_z - n_b
    rounds = n_c
    kinds = [
        (("z", "x", "y"), 0, n_b, 1),
        (("z", "y", "x"), n_b, n_c, 1),
        (("x", "y", "z"), n_b + n_c, n_last_z, 2),
    ]
    slots = {("up", s): s for s in range(depth - 1)}
    slots.update({("down", s): depth - 1 + s for s in range(depth - 1)})
    for name in ("x", "y", "core"):
        slots[name] = len(slots)

    def item(tap, held, **at):
        parts = [
            at.get(name, slice(None) if name in held else mine)
            for name, mine in (("z", pz), ("y", py), ("x", px), ("core", core))
        ]
        return whole.at[(tap, *parts)]

    def copy(kind, tap, what, target, slot):
        return pltpu.make_async_remote_copy(
            src_ref=what,
            dst_ref=what,
            send_sem=send_sem.at[kind, slots[slot]],
            recv_sem=recv_sem.at[0 if isinstance(tap, pl.Slice) else tap, slots[slot]],
            device_id={"tm": target},
            device_id_type=pl.DeviceIdType.MESH,
        )

    def steps_of(kind, order):
        sends, receives, waits = [], [], []
        held = ()

        def hop(name, held):
            other = {"x": 1 - px, "y": 1 - py, "core": 1 - core}[name]
            sends.append(
                [(None, lambda tap: copy(kind, tap, item(tap, held), neighbour[name], name))]
            )
            receives.append(
                [
                    (
                        None,
                        lambda tap: copy(
                            kind, tap, item(tap, held, **{name: other}), neighbour[name], name
                        ),
                    )
                ]
            )

        def line(step, held):
            def sent(way, sign):
                return lambda tap: copy(
                    kind, tap, item(tap, held, z=pz - sign * step), neighbour[way], (way, step)
                )

            def got(way, sign):
                return lambda tap: copy(
                    kind,
                    tap,
                    item(tap, held, z=pz - sign * (step + 1)),
                    neighbour["down" if way == "up" else "up"],
                    (way, step),
                )

            sends.append(
                [
                    ((pz < depth - 1) & (pz - step >= 0), sent("up", 1)),
                    ((pz > 0) & (pz + step <= depth - 1), sent("down", -1)),
                ]
            )
            receives.append(
                [
                    (pz - step - 1 >= 0, got("up", 1)),
                    (pz + step + 1 <= depth - 1, got("down", -1)),
                ]
            )

        for name in order + ("core",):
            if name == "z":
                for step in range(depth - 1):
                    line(step, held)
            else:
                hop(name, held)
            held = held + (name,)
        return sends, receives

    plans = [steps_of(kind, entry[0]) for kind, entry in enumerate(kinds)]
    stages = len(plans[0][0])

    def guarded(condition, action):
        if condition is None:
            action()
        else:
            pl.when(condition)(action)

    def tap_of(kind, r):
        order, first, count, every = kinds[kind]
        if every == 1:
            return first + r, (r >= 0) & (r < count)
        return first + lax.div(r, every), (r >= 0) & (r < count * every) & (lax.rem(r, every) == 0)

    def advance(tick, low, high):
        for stage in range(high - 1, low - 1, -1):
            for kind in range(len(kinds)):
                tap, valid = tap_of(kind, tick - stage)
                sends, receives = plans[kind]

                @pl.when(valid)
                def _():
                    if stage > 0:
                        for condition, make in receives[stage - 1]:
                            guarded(condition, lambda: make(tap).wait_recv())
                    if stage < stages:
                        for condition, make in sends[stage]:
                            guarded(condition, lambda: make(tap).start())

    def use_tap(tap):
        a = lax.div(tap, 9)
        b = lax.rem(lax.div(tap, 3), 3)
        e = lax.rem(tap, 3)
        weights = whole[tap].reshape(channels, channels)
        forward = act_wide[a, e, pl.ds(pl.multiple_of(b * columns, columns), cells)]
        conv_acc[...] += jnp.dot(forward, weights, preferred_element_type=jnp.float32)
        back = grad_wide[
            2 - a, 2 - e, pl.ds(pl.multiple_of((2 - b) * columns, columns), cells)
        ]
        grad_acc[...] += lax.dot_general(
            back, weights, (((1,), (1,)), ((), ())), preferred_element_type=jnp.float32
        )

    def compute(tick):
        for kind in range(len(kinds)):
            tap, valid = tap_of(kind, tick - stages)
            pl.when(valid)(functools.partial(use_tap, tap))

    def halo(source, target, place, slot):
        return pltpu.make_async_remote_copy(
            src_ref=source,
            dst_ref=place,
            send_sem=halo_send.at[slot],
            recv_sem=halo_recv.at[slot],
            device_id={"tm": target},
            device_id_type=pl.DeviceIdType.MESH,
        )

    own_act = act_halo.at[2]
    grad_copies = [
        (me > d, me < n - 1 - d, halo(grad_ref, me - 1 - d, grad_halo.at[d], d)) for d in range(2)
    ]
    act_copies = [
        (me < n - 1 - d, me > d, halo(own_act, me + 1 + d, act_halo.at[1 - d], 2 + d))
        for d in range(2)
    ]

    advance(0, 0, 1)
    for sends_it, _, this in grad_copies:
        pl.when(sends_it)(this.start)

    latent_wide = latent_ref[...].astype(jnp.float32)
    gain = gain_ref[...]
    count = cells * group
    average = group_mean(sums_of(latent_wide), group, count)
    centred = latent_wide - average
    spread = group_mean(sums_of(centred * centred), group, count)
    inverse = lax.rsqrt(spread + epsilon)
    inverse_ref[...] = inverse
    normed = centred * inverse
    normed_ref[...] = normed
    scaled = normed * gain
    activated = scaled * jax.nn.sigmoid(scaled)
    own_act[...] = activated.astype(jnp.bfloat16)
    for sends_it, _, this in act_copies:
        pl.when(sends_it)(this.start)
    conv_acc[...] = jnp.zeros_like(conv_acc)
    grad_acc[...] = jnp.zeros_like(grad_acc)

    def early(tick, carry):
        advance(tick, 0, stages)
        return carry

    lax.fori_loop(1, stages - 1, early, 0)

    column = lax.rem(lax.broadcasted_iota(jnp.int32, (cells, channels), 0), columns)
    edge = jnp.zeros((columns, channels), jnp.bfloat16)

    def widen(frame, wide, place):
        values = frame.astype(jnp.float32)
        left = jnp.where(column == 0, 0.0, pltpu.roll(values, 1, 0))
        right = jnp.where(column == columns - 1, 0.0, pltpu.roll(values, cells - 1, 0))
        for e, part in enumerate((left, values, right)):
            wide[place, e, 0:columns] = edge
            wide[place, e, columns : columns + cells] = part.astype(jnp.bfloat16)
            wide[place, e, columns + cells : 2 * columns + cells] = edge

    widen(act_halo[2], act_wide, 2)
    widen(grad_ref[...], grad_wide, 0)
    for d in range(2):
        for copies, buffer, wide, place, at in (
            (grad_copies, grad_halo, grad_wide, d + 1, d),
            (act_copies, act_halo, act_wide, 1 - d, 1 - d),
        ):
            _, gets_it, this = copies[d]
            pl.when(gets_it)(this.wait_recv)

            @pl.when(jnp.logical_not(gets_it))
            def _():
                buffer[at] = jnp.zeros((cells, channels), jnp.bfloat16)

            widen(buffer[at], wide, place)

    def late(tick, carry):
        advance(tick, 0, stages + 1)
        compute(tick)
        return carry

    lax.fori_loop(stages - 1, rounds + stages, late, 0)

    refined_ref[...] = (latent_ref[...].astype(jnp.float32) + conv_acc[...]).astype(jnp.bfloat16)
    normed = normed_ref[...]
    scaled = normed * gain
    s = jax.nn.sigmoid(scaled)
    grad_normed = grad_acc[...] * s * (1.0 + scaled * (1.0 - s)) * gain
    first = group_mean(sums_of(grad_normed), group, count)
    second = group_mean(sums_of(grad_normed * normed), group, count)
    out_ref[...] = grad_ref[...].astype(jnp.float32) + (
        grad_normed - first - normed * second
    ) * inverse_ref[...]

    for sends_it, _, this in grad_copies + act_copies:
        pl.when(sends_it)(this.wait_send)
    for kind, (order, first_tap, count_taps, _) in enumerate(kinds):
        for stage in plans[kind][0]:
            for condition, make in stage:
                guarded(
                    condition,
                    lambda: make(pl.ds(first_tap, count_taps)).wait_send(),
                )


def fused(latent, norm_gain, conv_weight, grad_out):
    n = lax.axis_size("tm")
    _, rows_here, columns, channels = latent.shape
    cells = rows_here * columns
    taps, depth = conv_weight.shape[:2]
    line = n // 8
    slots = 2 * (line - 1) + 3
    bf16, f32 = jnp.bfloat16, jnp.float32
    wide = (3, 3, cells + 2 * columns, channels)
    vmem = pl.BlockSpec(memory_space=pltpu.VMEM)
    refined, grad_latent = pl.pallas_call(
        functools.partial(block_kernel, n, columns),
        out_shape=(
            jax.ShapeDtypeStruct((cells, channels), bf16),
            jax.ShapeDtypeStruct((cells, channels), f32),
        ),
        in_specs=[vmem, vmem, pl.BlockSpec(memory_space=pl.ANY), vmem],
        out_specs=(vmem, vmem),
        scratch_shapes=[
            pltpu.VMEM((taps, line, 2, 2, 2, depth, channels), bf16),
            pltpu.VMEM((3, cells, channels), bf16),
            pltpu.VMEM((2, cells, channels), bf16),
            pltpu.VMEM(wide, bf16),
            pltpu.VMEM(wide, bf16),
            pltpu.VMEM((cells, channels), f32),
            pltpu.VMEM((1, channels), f32),
            pltpu.VMEM((cells, channels), f32),
            pltpu.VMEM((cells, channels), f32),
            pltpu.SemaphoreType.DMA,
            pltpu.SemaphoreType.DMA((3, slots)),
            pltpu.SemaphoreType.DMA((taps, slots)),
            pltpu.SemaphoreType.DMA((4,)),
            pltpu.SemaphoreType.DMA((4,)),
        ],
        compiler_params=pltpu.CompilerParams(
            collective_id=0, has_side_effects=True, vmem_limit_bytes=52 * 2**20
        ),
        cost_estimate=pl.CostEstimate(
            flops=4 * taps * cells * channels * channels,
            bytes_accessed=taps * channels * channels * 2,
            transcendentals=2 * cells * channels,
        ),
    )(
        latent.reshape(cells, channels),
        norm_gain.reshape(1, channels),
        conv_weight,
        grad_out.reshape(cells, channels),
    )
    return refined.reshape(latent.shape), grad_latent.reshape(latent.shape)


def shards(latent, norm_gain, conv_weight, grad_out):
    group = latent.shape[3] // GROUPS
    whole_frame = lax.axis_size("rows") == 1 and latent.shape[0] == 1
    if whole_frame and lax.axis_size("tm") % 8 == 0 and group & (group - 1) == 0:
        return fused(latent, norm_gain, conv_weight, grad_out)
    return general(latent, norm_gain, conv_weight, grad_out)


def general(latent, norm_gain, conv_weight, grad_out):
    frames_here, rows_here, columns, channels = latent.shape
    cell_count = lax.axis_size("rows") * rows_here * columns * (channels // GROUPS)
    full_weight = lax.all_gather(conv_weight, "tm", axis=1, tiled=True)
    latent_wide = latent.astype(jnp.float32)
    grouped = grouped_view(latent_wide)
    average = lax.psum(jnp.sum(grouped, axis=(1, 3)), "rows") / cell_count
    centred = grouped - average[:, None, :, None]
    spread = lax.psum(jnp.sum(centred * centred, axis=(1, 3)), "rows") / cell_count
    inverse = lax.rsqrt(spread + epsilon)
    normed_grouped = centred * inverse[:, None, :, None]
    normed = normed_grouped.reshape(latent.shape)
    scaled = normed * norm_gain
    sigmoid_value = jax.nn.sigmoid(scaled)
    activated = (scaled * sigmoid_value).astype(jnp.bfloat16)
    before_one = shifted(activated, "tm", 1)
    before_two = shifted(activated, "tm", 2)
    padded = with_halo(
        jnp.concatenate([before_two, before_one, activated], axis=0), (("rows", 1),), 1
    )
    after_one = shifted(grad_out, "tm", -1)
    after_two = shifted(grad_out, "tm", -2)
    padded_grad = with_halo(
        jnp.concatenate([grad_out, after_one, after_two], axis=0), (("rows", 1),), 1
    )
    padded = widen_columns(padded)
    padded_grad = widen_columns(padded_grad)
    conv_sum = jnp.zeros((frames_here * rows_here * columns, channels), jnp.float32)
    grad_act = jnp.zeros((frames_here * rows_here * columns, channels), jnp.float32)
    for time_tap in range(3):
        for row_tap in range(3):
            for col_tap in range(3):
                tap_weight = full_weight[time_tap * 9 + row_tap * 3 + col_tap]
                window = padded[
                    time_tap : time_tap + frames_here,
                    row_tap : row_tap + rows_here,
                    col_tap : col_tap + columns,
                ]
                conv_sum = conv_sum + jnp.dot(
                    window.reshape(-1, channels), tap_weight, preferred_element_type=jnp.float32
                )
                back_window = padded_grad[
                    2 - time_tap : 2 - time_tap + frames_here,
                    2 - row_tap : 2 - row_tap + rows_here,
                    2 - col_tap : 2 - col_tap + columns,
                ]
                grad_act = grad_act + lax.dot_general(
                    back_window.reshape(-1, channels),
                    tap_weight,
                    (((1,), (1,)), ((), ())),
                    preferred_element_type=jnp.float32,
                )
    refined = (latent_wide + conv_sum.reshape(latent.shape)).astype(jnp.bfloat16)
    grad_scaled = (
        grad_act.reshape(latent.shape) * sigmoid_value * (1.0 + scaled * (1.0 - sigmoid_value))
    )
    grad_normed = grouped_view(grad_scaled * norm_gain)
    first_sum, second_sum = lax.psum(
        (jnp.sum(grad_normed, axis=(1, 3)), jnp.sum(grad_normed * normed_grouped, axis=(1, 3))),
        "rows",
    )
    first = first_sum / cell_count
    second = second_sum / cell_count
    grad_norm_part = (
        grad_normed - first[:, None, :, None] - normed_grouped * second[:, None, :, None]
    ) * inverse[:, None, :, None]
    grad_latent = grad_out.astype(jnp.float32) + grad_norm_part.reshape(latent.shape)
    return (refined, grad_latent)


def solution(mesh):
    placed = (P("tm", "rows", None, None), P(), P(None, "tm", None), P("tm", "rows", None, None))
    return jax.shard_map(
        shards,
        mesh=mesh,
        in_specs=placed,
        out_specs=(P("tm", "rows", None, None), P("tm", "rows", None, None)),
        check_vma=False,
    )
```

```python
import functools

import jax
import jax.numpy as jnp
from jax import lax
from jax.experimental import pallas as pl
from jax.experimental.pallas import tpu as pltpu
from jax.sharding import PartitionSpec as P

GROUPS = 32


epsilon = 1e-06


def shifted(block, axis, distance):
    devices = range(lax.axis_size(axis))
    route = [(i - distance, i) for i in devices if i - distance in devices]
    return lax.ppermute(block, axis, route)


def with_halo(shard, sides, width):
    for axis, dim in sides:
        size, length = (lax.axis_size(axis), shard.shape[dim])
        up = [(i, (i + 1) % size) for i in range(size - 1)]
        down = [(j, i) for i, j in up]
        last = lax.slice_in_dim(shard, length - width, length, axis=dim)
        first = lax.slice_in_dim(shard, 0, width, axis=dim)
        before = lax.ppermute(last, axis, up)
        after = lax.ppermute(first, axis, down)
        shard = jnp.concatenate([before, shard, after], axis=dim)
    return shard


def grouped_view(values):
    return values.reshape(
        values.shape[0], values.shape[1] * values.shape[2], GROUPS, values.shape[3] // GROUPS
    )


def widen_columns(values):
    return jnp.pad(values, ((0, 0), (0, 0), (1, 1), (0, 0)))


def group_mean(row, group, cells):
    channels = row.shape[1]
    shift = group.bit_length() - 1
    shape = (channels, channels)
    left = lax.shift_right_logical(lax.broadcasted_iota(jnp.int32, shape, 0), shift)
    right = lax.shift_right_logical(lax.broadcasted_iota(jnp.int32, shape, 1), shift)
    same = jnp.where(left == right, 1.0, 0.0).astype(jnp.float32)
    wide = jnp.broadcast_to(row, (8, channels))
    sums = jnp.dot(
        wide, same, preferred_element_type=jnp.float32, precision=lax.Precision.HIGHEST
    )
    return sums[0:1] / cells


def sums_of(values):
    return jnp.sum(values, axis=0, keepdims=True)


def block_kernel(
    n,
    columns,
    latent_hbm,
    gain_hbm,
    weight_ref,
    grad_hbm,
    refined_ref,
    out_ref,
    latent_ref,
    gain_ref,
    grad_ref,
    whole,
    act_halo,
    grad_halo,
    act_wide,
    grad_wide,
    normed_ref,
    inverse_ref,
    conv_acc,
    grad_acc,
    own_sem,
    fetch_sem,
    send_sem,
    recv_sem,
    halo_send,
    halo_recv,
):
    me = lax.axis_index("tm")
    depth = n // 8
    core = lax.rem(me, 2)
    px = lax.rem(lax.div(me, 2), 2)
    py = lax.rem(lax.div(me, 4), 2)
    pz = lax.div(me, 8)
    cells, channels = latent_ref.shape
    taps = weight_ref.shape[0]
    group = channels // GROUPS
    neighbour = {
        "x": me + 2 - 4 * px,
        "y": me + 4 - 8 * py,
        "core": me + 1 - 2 * core,
        "up": me + 8,
        "down": me - 8,
    }

    own_copy = pltpu.make_async_copy(weight_ref, whole.at[:, pz, py, px, core], own_sem)
    own_copy.start()
    fetches = [
        pltpu.make_async_copy(source, place, fetch_sem.at[i])
        for i, (source, place) in enumerate(
            ((grad_hbm, grad_ref), (latent_hbm, latent_ref), (gain_hbm, gain_ref))
        )
    ]
    for fetch in fetches:
        fetch.start()

    barrier = pltpu.get_barrier_semaphore()

    def greet(other):
        pl.semaphore_signal(
            barrier, inc=1, device_id={"tm": other}, device_id_type=pl.DeviceIdType.MESH
        )

    for name in ("x", "y", "core"):
        greet(neighbour[name])
    linked = [
        (pz < depth - 1, me + 8),
        (pz > 0, me - 8),
        (me < n - 1, me + 1),
        (me < n - 2, me + 2),
        (me > 0, me - 1),
        (me > 1, me - 2),
    ]
    expected = jnp.int32(3)
    for there, other in linked:
        pl.when(there)(functools.partial(greet, other))
        expected = expected + there.astype(jnp.int32)
    own_copy.wait()
    pl.semaphore_wait(barrier, expected)

    n_last_z = (2 * taps) // 9
    n_b = (taps - n_last_z) // 2
    n_c = taps - n_last_z - n_b
    rounds = n_c
    lag = 2
    kinds = [
        (("z", "x", "y"), 0, n_b, 1),
        (("z", "y", "x"), n_b, n_c, 1),
        (("x", "y", "z"), n_b + n_c, n_last_z, 2),
    ]
    slots = {("up", s): s for s in range(depth - 1)}
    slots.update({("down", s): depth - 1 + s for s in range(depth - 1)})
    for name in ("x", "y", "core"):
        slots[name] = len(slots)

    def item(tap, held, **at):
        parts = [
            at.get(name, slice(None) if name in held else mine)
            for name, mine in (("z", pz), ("y", py), ("x", px), ("core", core))
        ]
        return whole.at[(tap, *parts)]

    def copy(kind, tap, what, target, slot):
        return pltpu.make_async_remote_copy(
            src_ref=what,
            dst_ref=what,
            send_sem=send_sem.at[kind, slots[slot]],
            recv_sem=recv_sem.at[0 if isinstance(tap, pl.Slice) else tap, slots[slot]],
            device_id={"tm": target},
            device_id_type=pl.DeviceIdType.MESH,
        )

    def steps_of(kind, order):
        sends, receives, waits = [], [], []
        held = ()

        def hop(name, held):
            other = {"x": 1 - px, "y": 1 - py, "core": 1 - core}[name]
            sends.append(
                [(None, lambda tap: copy(kind, tap, item(tap, held), neighbour[name], name))]
            )
            receives.append(
                [
                    (
                        None,
                        lambda tap: copy(
                            kind, tap, item(tap, held, **{name: other}), neighbour[name], name
                        ),
                    )
                ]
            )

        def line(step, held):
            def sent(way, sign):
                return lambda tap: copy(
                    kind, tap, item(tap, held, z=pz - sign * step), neighbour[way], (way, step)
                )

            def got(way, sign):
                return lambda tap: copy(
                    kind,
                    tap,
                    item(tap, held, z=pz - sign * (step + 1)),
                    neighbour["down" if way == "up" else "up"],
                    (way, step),
                )

            sends.append(
                [
                    ((pz < depth - 1) & (pz - step >= 0), sent("up", 1)),
                    ((pz > 0) & (pz + step <= depth - 1), sent("down", -1)),
                ]
            )
            receives.append(
                [
                    (pz - step - 1 >= 0, got("up", 1)),
                    (pz + step + 1 <= depth - 1, got("down", -1)),
                ]
            )

        for name in order + ("core",):
            if name == "z":
                for step in range(depth - 1):
                    line(step, held)
            else:
                hop(name, held)
            held = held + (name,)
        return sends, receives

    plans = [steps_of(kind, entry[0]) for kind, entry in enumerate(kinds)]
    stages = len(plans[0][0])

    def guarded(condition, action):
        if condition is None:
            action()
        else:
            pl.when(condition)(action)

    def tap_of(kind, r):
        order, first, count, every = kinds[kind]
        if every == 1:
            return first + r, (r >= 0) & (r < count)
        return first + lax.div(r, every), (r >= 0) & (r < count * every) & (lax.rem(r, every) == 0)

    def advance(tick, low, high):
        for stage in range(high - 1, low - 1, -1):
            for kind in range(len(kinds)):
                tap, valid = tap_of(kind, tick - lag * stage)
                sends, receives = plans[kind]

                @pl.when(valid)
                def _():
                    if stage > 0:
                        for condition, make in receives[stage - 1]:
                            guarded(condition, lambda: make(tap).wait_recv())
                    if stage < stages:
                        for condition, make in sends[stage]:
                            guarded(condition, lambda: make(tap).start())

    def use_tap(tap):
        a = lax.div(tap, 9)
        b = lax.rem(lax.div(tap, 3), 3)
        e = lax.rem(tap, 3)
        weights = whole[tap].reshape(channels, channels)
        forward = act_wide[a, e, pl.ds(pl.multiple_of(b * columns, columns), cells)]
        conv_acc[...] += jnp.dot(forward, weights, preferred_element_type=jnp.float32)
        back = grad_wide[
            2 - a, 2 - e, pl.ds(pl.multiple_of((2 - b) * columns, columns), cells)
        ]
        grad_acc[...] += lax.dot_general(
            back, weights, (((1,), (1,)), ((), ())), preferred_element_type=jnp.float32
        )

    def compute(tick):
        for kind in range(len(kinds)):
            tap, valid = tap_of(kind, tick - lag * stages)
            pl.when(valid)(functools.partial(use_tap, tap))

    def halo(source, target, place, slot):
        return pltpu.make_async_remote_copy(
            src_ref=source,
            dst_ref=place,
            send_sem=halo_send.at[slot],
            recv_sem=halo_recv.at[slot],
            device_id={"tm": target},
            device_id_type=pl.DeviceIdType.MESH,
        )

    own_act = act_halo.at[2]
    grad_copies = [
        (me > d, me < n - 1 - d, halo(grad_ref, me - 1 - d, grad_halo.at[d], d)) for d in range(2)
    ]
    act_copies = [
        (me < n - 1 - d, me > d, halo(own_act, me + 1 + d, act_halo.at[1 - d], 2 + d))
        for d in range(2)
    ]

    for tick in range(lag):
        advance(tick, 0, 1)
    for fetch in fetches:
        fetch.wait()
    for sends_it, _, this in grad_copies:
        pl.when(sends_it)(this.start)

    latent_wide = latent_ref[...].astype(jnp.float32)
    gain = gain_ref[...]
    count = cells * group
    average = group_mean(sums_of(latent_wide), group, count)
    centred = latent_wide - average
    spread = group_mean(sums_of(centred * centred), group, count)
    inverse = lax.rsqrt(spread + epsilon)
    inverse_ref[...] = inverse
    normed = centred * inverse
    normed_ref[...] = normed
    scaled = normed * gain
    activated = scaled * jax.nn.sigmoid(scaled)
    own_act[...] = activated.astype(jnp.bfloat16)
    for sends_it, _, this in act_copies:
        pl.when(sends_it)(this.start)
    conv_acc[...] = jnp.zeros_like(conv_acc)
    grad_acc[...] = jnp.zeros_like(grad_acc)

    column = lax.rem(lax.broadcasted_iota(jnp.int32, (cells, channels), 0), columns)
    edge = jnp.zeros((columns, channels), jnp.bfloat16)

    def widen(frame, wide, place):
        values = frame.astype(jnp.float32)
        left = jnp.where(column == 0, 0.0, pltpu.roll(values, 1, 0))
        right = jnp.where(column == columns - 1, 0.0, pltpu.roll(values, cells - 1, 0))
        for e, part in enumerate((left, values, right)):
            wide[place, e, 0:columns] = edge
            wide[place, e, columns : columns + cells] = part.astype(jnp.bfloat16)
            wide[place, e, columns + cells : 2 * columns + cells] = edge

    def take(copies, d, buffer, at, wide, place):
        _, gets_it, this = copies[d]
        pl.when(gets_it)(this.wait_recv)

        @pl.when(jnp.logical_not(gets_it))
        def _():
            buffer[at] = jnp.zeros((cells, channels), jnp.bfloat16)

        widen(buffer[at], wide, place)

    jobs = [
        lambda: widen(act_halo[2], act_wide, 2),
        lambda: widen(grad_ref[...], grad_wide, 0),
        lambda: take(grad_copies, 0, grad_halo, 0, grad_wide, 1),
        lambda: take(act_copies, 0, act_halo, 1, act_wide, 1),
        lambda: take(grad_copies, 1, grad_halo, 1, grad_wide, 2),
        lambda: take(act_copies, 1, act_halo, 0, act_wide, 0),
    ]

    def early(tick, carry):
        advance(tick, 0, stages)
        for i, job in enumerate(jobs):
            pl.when(tick == lag + 1 + i)(job)
        return carry

    lax.fori_loop(lag, lag * stages - 1, early, 0)

    def late(tick, carry):
        advance(tick, 0, stages + 1)
        compute(tick)
        return carry

    lax.fori_loop(lag * stages - 1, rounds + lag * stages, late, 0)

    refined_ref[...] = (latent_ref[...].astype(jnp.float32) + conv_acc[...]).astype(jnp.bfloat16)
    normed = normed_ref[...]
    scaled = normed * gain
    s = jax.nn.sigmoid(scaled)
    grad_normed = grad_acc[...] * s * (1.0 + scaled * (1.0 - s)) * gain
    first = group_mean(sums_of(grad_normed), group, count)
    second = group_mean(sums_of(grad_normed * normed), group, count)
    out_ref[...] = grad_ref[...].astype(jnp.float32) + (
        grad_normed - first - normed * second
    ) * inverse_ref[...]

    for sends_it, _, this in grad_copies + act_copies:
        pl.when(sends_it)(this.wait_send)
    for kind, (order, first_tap, count_taps, _) in enumerate(kinds):
        for stage in plans[kind][0]:
            for condition, make in stage:
                guarded(
                    condition,
                    lambda: make(pl.ds(first_tap, count_taps)).wait_send(),
                )


def fused(latent, norm_gain, conv_weight, grad_out):
    n = lax.axis_size("tm")
    _, rows_here, columns, channels = latent.shape
    cells = rows_here * columns
    taps, depth = conv_weight.shape[:2]
    line = n // 8
    slots = 2 * (line - 1) + 3
    bf16, f32 = jnp.bfloat16, jnp.float32
    wide = (3, 3, cells + 2 * columns, channels)
    vmem = pl.BlockSpec(memory_space=pltpu.VMEM)
    far = pl.BlockSpec(memory_space=pltpu.HBM)
    refined, grad_latent = pl.pallas_call(
        functools.partial(block_kernel, n, columns),
        out_shape=(
            jax.ShapeDtypeStruct((cells, channels), bf16),
            jax.ShapeDtypeStruct((cells, channels), f32),
        ),
        in_specs=[far] * 4,
        out_specs=(vmem, vmem),
        scratch_shapes=[
            pltpu.VMEM((cells, channels), bf16),
            pltpu.VMEM((1, channels), f32),
            pltpu.VMEM((cells, channels), bf16),
            pltpu.VMEM((taps, line, 2, 2, 2, depth, channels), bf16),
            pltpu.VMEM((3, cells, channels), bf16),
            pltpu.VMEM((2, cells, channels), bf16),
            pltpu.VMEM(wide, bf16),
            pltpu.VMEM(wide, bf16),
            pltpu.VMEM((cells, channels), f32),
            pltpu.VMEM((1, channels), f32),
            pltpu.VMEM((cells, channels), f32),
            pltpu.VMEM((cells, channels), f32),
            pltpu.SemaphoreType.DMA,
            pltpu.SemaphoreType.DMA((3,)),
            pltpu.SemaphoreType.DMA((3, slots)),
            pltpu.SemaphoreType.DMA((taps, slots)),
            pltpu.SemaphoreType.DMA((4,)),
            pltpu.SemaphoreType.DMA((4,)),
        ],
        compiler_params=pltpu.CompilerParams(
            collective_id=0, has_side_effects=True, vmem_limit_bytes=64 * 2**20 - 2**17
        ),
        cost_estimate=pl.CostEstimate(
            flops=4 * taps * cells * channels * channels,
            bytes_accessed=taps * channels * channels * 2,
            transcendentals=2 * cells * channels,
        ),
    )(
        latent.reshape(cells, channels),
        norm_gain.reshape(1, channels),
        conv_weight,
        grad_out.reshape(cells, channels),
    )
    return refined.reshape(latent.shape), grad_latent.reshape(latent.shape)


def shards(latent, norm_gain, conv_weight, grad_out):
    group = latent.shape[3] // GROUPS
    whole_frame = lax.axis_size("rows") == 1 and latent.shape[0] == 1
    if whole_frame and lax.axis_size("tm") % 8 == 0 and group & (group - 1) == 0:
        return fused(latent, norm_gain, conv_weight, grad_out)
    return general(latent, norm_gain, conv_weight, grad_out)


def general(latent, norm_gain, conv_weight, grad_out):
    frames_here, rows_here, columns, channels = latent.shape
    cell_count = lax.axis_size("rows") * rows_here * columns * (channels // GROUPS)
    full_weight = lax.all_gather(conv_weight, "tm", axis=1, tiled=True)
    latent_wide = latent.astype(jnp.float32)
    grouped = grouped_view(latent_wide)
    average = lax.psum(jnp.sum(grouped, axis=(1, 3)), "rows") / cell_count
    centred = grouped - average[:, None, :, None]
    spread = lax.psum(jnp.sum(centred * centred, axis=(1, 3)), "rows") / cell_count
    inverse = lax.rsqrt(spread + epsilon)
    normed_grouped = centred * inverse[:, None, :, None]
    normed = normed_grouped.reshape(latent.shape)
    scaled = normed * norm_gain
    sigmoid_value = jax.nn.sigmoid(scaled)
    activated = (scaled * sigmoid_value).astype(jnp.bfloat16)
    before_one = shifted(activated, "tm", 1)
    before_two = shifted(activated, "tm", 2)
    padded = with_halo(
        jnp.concatenate([before_two, before_one, activated], axis=0), (("rows", 1),), 1
    )
    after_one = shifted(grad_out, "tm", -1)
    after_two = shifted(grad_out, "tm", -2)
    padded_grad = with_halo(
        jnp.concatenate([grad_out, after_one, after_two], axis=0), (("rows", 1),), 1
    )
    padded = widen_columns(padded)
    padded_grad = widen_columns(padded_grad)
    conv_sum = jnp.zeros((frames_here * rows_here * columns, channels), jnp.float32)
    grad_act = jnp.zeros((frames_here * rows_here * columns, channels), jnp.float32)
    for time_tap in range(3):
        for row_tap in range(3):
            for col_tap in range(3):
                tap_weight = full_weight[time_tap * 9 + row_tap * 3 + col_tap]
                window = padded[
                    time_tap : time_tap + frames_here,
                    row_tap : row_tap + rows_here,
                    col_tap : col_tap + columns,
                ]
                conv_sum = conv_sum + jnp.dot(
                    window.reshape(-1, channels), tap_weight, preferred_element_type=jnp.float32
                )
                back_window = padded_grad[
                    2 - time_tap : 2 - time_tap + frames_here,
                    2 - row_tap : 2 - row_tap + rows_here,
                    2 - col_tap : 2 - col_tap + columns,
                ]
                grad_act = grad_act + lax.dot_general(
                    back_window.reshape(-1, channels),
                    tap_weight,
                    (((1,), (1,)), ((), ())),
                    preferred_element_type=jnp.float32,
                )
    refined = (latent_wide + conv_sum.reshape(latent.shape)).astype(jnp.bfloat16)
    grad_scaled = (
        grad_act.reshape(latent.shape) * sigmoid_value * (1.0 + scaled * (1.0 - sigmoid_value))
    )
    grad_normed = grouped_view(grad_scaled * norm_gain)
    first_sum, second_sum = lax.psum(
        (jnp.sum(grad_normed, axis=(1, 3)), jnp.sum(grad_normed * normed_grouped, axis=(1, 3))),
        "rows",
    )
    first = first_sum / cell_count
    second = second_sum / cell_count
    grad_norm_part = (
        grad_normed - first[:, None, :, None] - normed_grouped * second[:, None, :, None]
    ) * inverse[:, None, :, None]
    grad_latent = grad_out.astype(jnp.float32) + grad_norm_part.reshape(latent.shape)
    return (refined, grad_latent)


def solution(mesh):
    placed = (P("tm", "rows", None, None), P(), P(None, "tm", None), P("tm", "rows", None, None))
    return jax.shard_map(
        shards,
        mesh=mesh,
        in_specs=placed,
        out_specs=(P("tm", "rows", None, None), P("tm", "rows", None, None)),
        check_vma=False,
    )
```

```python
import functools

import jax
import jax.numpy as jnp
from jax import lax
from jax.experimental import pallas as pl
from jax.experimental.pallas import tpu as pltpu
from jax.sharding import PartitionSpec as P

GROUPS = 32


epsilon = 1e-06


def shifted(block, axis, distance):
    devices = range(lax.axis_size(axis))
    route = [(i - distance, i) for i in devices if i - distance in devices]
    return lax.ppermute(block, axis, route)


def with_halo(shard, sides, width):
    for axis, dim in sides:
        size, length = (lax.axis_size(axis), shard.shape[dim])
        up = [(i, (i + 1) % size) for i in range(size - 1)]
        down = [(j, i) for i, j in up]
        last = lax.slice_in_dim(shard, length - width, length, axis=dim)
        first = lax.slice_in_dim(shard, 0, width, axis=dim)
        before = lax.ppermute(last, axis, up)
        after = lax.ppermute(first, axis, down)
        shard = jnp.concatenate([before, shard, after], axis=dim)
    return shard


def grouped_view(values):
    return values.reshape(
        values.shape[0], values.shape[1] * values.shape[2], GROUPS, values.shape[3] // GROUPS
    )


def widen_columns(values):
    return jnp.pad(values, ((0, 0), (0, 0), (1, 1), (0, 0)))


def group_mean(row, group, cells):
    channels = row.shape[1]
    shift = group.bit_length() - 1
    shape = (channels, channels)
    left = lax.shift_right_logical(lax.broadcasted_iota(jnp.int32, shape, 0), shift)
    right = lax.shift_right_logical(lax.broadcasted_iota(jnp.int32, shape, 1), shift)
    same = jnp.where(left == right, 1.0, 0.0).astype(jnp.float32)
    wide = jnp.broadcast_to(row, (8, channels))
    sums = jnp.dot(
        wide, same, preferred_element_type=jnp.float32, precision=lax.Precision.HIGHEST
    )
    return sums[0:1] / cells


def sums_of(values):
    return jnp.sum(values, axis=0, keepdims=True)


def block_kernel(
    n,
    columns,
    latent_hbm,
    gain_hbm,
    weight_ref,
    grad_hbm,
    refined_ref,
    out_ref,
    latent_ref,
    gain_ref,
    grad_ref,
    whole,
    act_halo,
    grad_halo,
    act_wide,
    grad_wide,
    normed_ref,
    inverse_ref,
    conv_acc,
    grad_acc,
    own_sem,
    fetch_sem,
    send_sem,
    recv_sem,
    halo_send,
    halo_recv,
):
    me = lax.axis_index("tm")
    depth = n // 8
    core = lax.rem(me, 2)
    px = lax.rem(lax.div(me, 2), 2)
    py = lax.rem(lax.div(me, 4), 2)
    pz = lax.div(me, 8)
    cells, channels = latent_ref.shape
    taps = weight_ref.shape[0]
    group = channels // GROUPS
    neighbour = {
        "x": me + 2 - 4 * px,
        "y": me + 4 - 8 * py,
        "core": me + 1 - 2 * core,
        "up": me + 8,
        "down": me - 8,
    }

    own_copy = pltpu.make_async_copy(weight_ref, whole.at[:, pz, py, px, core], own_sem)
    own_copy.start()
    fetches = [
        pltpu.make_async_copy(source, place, fetch_sem.at[i])
        for i, (source, place) in enumerate(
            ((grad_hbm, grad_ref), (latent_hbm, latent_ref), (gain_hbm, gain_ref))
        )
    ]
    for fetch in fetches:
        fetch.start()

    barrier = pltpu.get_barrier_semaphore()

    def greet(other):
        pl.semaphore_signal(
            barrier, inc=1, device_id={"tm": other}, device_id_type=pl.DeviceIdType.MESH
        )

    for name in ("x", "y", "core"):
        greet(neighbour[name])
    linked = [
        (pz < depth - 1, me + 8),
        (pz > 0, me - 8),
        (me < n - 1, me + 1),
        (me < n - 2, me + 2),
        (me > 0, me - 1),
        (me > 1, me - 2),
    ]
    expected = jnp.int32(3)
    for there, other in linked:
        pl.when(there)(functools.partial(greet, other))
        expected = expected + there.astype(jnp.int32)
    own_copy.wait()
    pl.semaphore_wait(barrier, expected)

    n_last_z = (taps + 1) // 4
    n_b = (taps - n_last_z) // 2
    n_c = taps - n_last_z - n_b
    rounds = n_c
    line_first = (*range(depth), depth + 1, depth + 3, depth + 4)
    line_last = (0, 1, *range(2, 2 * depth + 1, 2), 2 * depth + 1)
    kinds = [
        (("z", "x", "y"), 0, n_b, line_first),
        (("z", "y", "x"), n_b, n_c, line_first),
        (("x", "y", "z"), n_b + n_c, n_last_z, line_last),
    ]
    slots = {("up", s): s for s in range(depth - 1)}
    slots.update({("down", s): depth - 1 + s for s in range(depth - 1)})
    for name in ("x", "y", "core"):
        slots[name] = len(slots)

    def item(tap, held, **at):
        parts = [
            at.get(name, slice(None) if name in held else mine)
            for name, mine in (("z", pz), ("y", py), ("x", px), ("core", core))
        ]
        return whole.at[(tap, *parts)]

    def copy(kind, tap, what, target, slot):
        return pltpu.make_async_remote_copy(
            src_ref=what,
            dst_ref=what,
            send_sem=send_sem.at[kind, slots[slot]],
            recv_sem=recv_sem.at[0 if isinstance(tap, pl.Slice) else tap, slots[slot]],
            device_id={"tm": target},
            device_id_type=pl.DeviceIdType.MESH,
        )

    def steps_of(kind, order):
        sends, receives, waits = [], [], []
        held = ()

        def hop(name, held):
            other = {"x": 1 - px, "y": 1 - py, "core": 1 - core}[name]
            sends.append(
                [(None, lambda tap: copy(kind, tap, item(tap, held), neighbour[name], name))]
            )
            receives.append(
                [
                    (
                        None,
                        lambda tap: copy(
                            kind, tap, item(tap, held, **{name: other}), neighbour[name], name
                        ),
                    )
                ]
            )

        def line(step, held):
            def sent(way, sign):
                return lambda tap: copy(
                    kind, tap, item(tap, held, z=pz - sign * step), neighbour[way], (way, step)
                )

            def got(way, sign):
                return lambda tap: copy(
                    kind,
                    tap,
                    item(tap, held, z=pz - sign * (step + 1)),
                    neighbour["down" if way == "up" else "up"],
                    (way, step),
                )

            sends.append(
                [
                    ((pz < depth - 1) & (pz - step >= 0), sent("up", 1)),
                    ((pz > 0) & (pz + step <= depth - 1), sent("down", -1)),
                ]
            )
            receives.append(
                [
                    (pz - step - 1 >= 0, got("up", 1)),
                    (pz + step + 1 <= depth - 1, got("down", -1)),
                ]
            )

        for name in order + ("core",):
            if name == "z":
                for step in range(depth - 1):
                    line(step, held)
            else:
                hop(name, held)
            held = held + (name,)
        return sends, receives

    plans = [steps_of(kind, entry[0]) for kind, entry in enumerate(kinds)]
    stages = len(plans[0][0])

    def guarded(condition, action):
        if condition is None:
            action()
        else:
            pl.when(condition)(action)

    def tap_of(kind, r):
        _, first, count, _ = kinds[kind]
        if count >= rounds - 1:
            return first + r, (r >= 0) & (r < count)
        spread_out = r * count
        return (
            first + lax.div(spread_out, rounds),
            (r >= 0) & (r < rounds) & (lax.rem(spread_out, rounds) < count),
        )

    def advance(tick, low, high):
        for stage in range(high - 1, low - 1, -1):
            for kind in range(len(kinds)):
                tap, valid = tap_of(kind, tick - kinds[kind][3][stage])
                sends, receives = plans[kind]

                @pl.when(valid)
                def _():
                    if stage > 0:
                        for condition, make in receives[stage - 1]:
                            guarded(condition, lambda: make(tap).wait_recv())
                    if stage < stages:
                        for condition, make in sends[stage]:
                            guarded(condition, lambda: make(tap).start())

    def use_tap(tap):
        a = lax.div(tap, 9)
        b = lax.rem(lax.div(tap, 3), 3)
        e = lax.rem(tap, 3)
        weights = whole[tap].reshape(channels, channels)
        forward = act_wide[a, e, pl.ds(pl.multiple_of(b * columns, columns), cells)]
        conv_acc[...] += jnp.dot(forward, weights, preferred_element_type=jnp.float32)
        back = grad_wide[
            2 - a, 2 - e, pl.ds(pl.multiple_of((2 - b) * columns, columns), cells)
        ]
        grad_acc[...] += lax.dot_general(
            back, weights, (((1,), (1,)), ((), ())), preferred_element_type=jnp.float32
        )

    def compute(tick):
        for kind in range(len(kinds)):
            tap, valid = tap_of(kind, tick - kinds[kind][3][stages])
            pl.when(valid)(functools.partial(use_tap, tap))

    def halo(source, target, place, slot, again=0):
        return pltpu.make_async_remote_copy(
            src_ref=source,
            dst_ref=place,
            send_sem=halo_send.at[slot + again],
            recv_sem=halo_recv.at[slot],
            device_id={"tm": target},
            device_id_type=pl.DeviceIdType.MESH,
        )

    own_act = act_halo.at[2]
    grad_copies = [
        (me > 0, me < n - 1, halo(grad_ref, me - 1, grad_halo.at[0], 0)),
        ((me > 1) & (core == 1), me < n - 2, halo(grad_ref, me - 2, grad_halo.at[1], 1)),
    ]
    act_copies = [
        (me < n - 1, me > 0, halo(own_act, me + 1, act_halo.at[1], 2)),
        ((me < n - 2) & (core == 0), me > 1, halo(own_act, me + 2, act_halo.at[0], 3)),
    ]
    passed_on = [
        ((me < n - 2) & (core == 1), halo(grad_halo.at[0], me - 1, grad_halo.at[1], 1, 4)),
        ((me > 1) & (core == 0), halo(act_halo.at[1], me + 1, act_halo.at[0], 3, 4)),
    ]

    advance(0, 0, 1)
    for fetch in fetches:
        fetch.wait()
    for sends_it, _, this in grad_copies:
        pl.when(sends_it)(this.start)

    latent_wide = latent_ref[...].astype(jnp.float32)
    gain = gain_ref[...]
    count = cells * group
    average = group_mean(sums_of(latent_wide), group, count)
    centred = latent_wide - average
    spread = group_mean(sums_of(centred * centred), group, count)
    inverse = lax.rsqrt(spread + epsilon)
    inverse_ref[...] = inverse
    normed = centred * inverse
    normed_ref[...] = normed
    scaled = normed * gain
    activated = scaled * jax.nn.sigmoid(scaled)
    own_act[...] = activated.astype(jnp.bfloat16)
    for sends_it, _, this in act_copies:
        pl.when(sends_it)(this.start)
    conv_acc[...] = jnp.zeros_like(conv_acc)
    grad_acc[...] = jnp.zeros_like(grad_acc)

    column = lax.rem(lax.broadcasted_iota(jnp.int32, (cells, channels), 0), columns)
    edge = jnp.zeros((columns, channels), jnp.bfloat16)

    def widen(frame, wide, place):
        values = frame.astype(jnp.float32)
        left = jnp.where(column == 0, 0.0, pltpu.roll(values, 1, 0))
        right = jnp.where(column == columns - 1, 0.0, pltpu.roll(values, cells - 1, 0))
        for e, part in enumerate((left, values, right)):
            wide[place, e, 0:columns] = edge
            wide[place, e, columns : columns + cells] = part.astype(jnp.bfloat16)
            wide[place, e, columns + cells : 2 * columns + cells] = edge

    def take(copies, d, buffer, at, wide, place):
        _, gets_it, this = copies[d]
        pl.when(gets_it)(this.wait_recv)
        if d == 0:
            passes, onward = passed_on[copies is act_copies]
            pl.when(passes)(onward.start)

        @pl.when(jnp.logical_not(gets_it))
        def _():
            buffer[at] = jnp.zeros((cells, channels), jnp.bfloat16)

        widen(buffer[at], wide, place)

    jobs = [
        lambda: widen(act_halo[2], act_wide, 2),
        lambda: widen(grad_ref[...], grad_wide, 0),
        lambda: take(grad_copies, 0, grad_halo, 0, grad_wide, 1),
        lambda: take(act_copies, 0, act_halo, 1, act_wide, 1),
        lambda: take(grad_copies, 1, grad_halo, 1, grad_wide, 2),
        lambda: take(act_copies, 1, act_halo, 0, act_wide, 0),
    ]

    def early(tick, carry):
        advance(tick, 0, stages)
        for i, job in enumerate(jobs):
            pl.when(tick == 1 + i)(job)
        return carry

    first_use = min(entry[3][stages] for entry in kinds)
    last_use = max(entry[3][stages] for entry in kinds)
    lax.fori_loop(1, first_use, early, 0)

    def late(tick, carry):
        advance(tick, 0, stages + 1)
        compute(tick)
        return carry

    lax.fori_loop(first_use, rounds + last_use, late, 0)

    refined_ref[...] = (latent_ref[...].astype(jnp.float32) + conv_acc[...]).astype(jnp.bfloat16)
    normed = normed_ref[...]
    scaled = normed * gain
    s = jax.nn.sigmoid(scaled)
    grad_normed = grad_acc[...] * s * (1.0 + scaled * (1.0 - s)) * gain
    first = group_mean(sums_of(grad_normed), group, count)
    second = group_mean(sums_of(grad_normed * normed), group, count)
    out_ref[...] = grad_ref[...].astype(jnp.float32) + (
        grad_normed - first - normed * second
    ) * inverse_ref[...]

    for sends_it, _, this in grad_copies + act_copies:
        pl.when(sends_it)(this.wait_send)
    for passes, onward in passed_on:
        pl.when(passes)(onward.wait_send)
    for kind, (order, first_tap, count_taps, _) in enumerate(kinds):
        for stage in plans[kind][0]:
            for condition, make in stage:
                guarded(
                    condition,
                    lambda: make(pl.ds(first_tap, count_taps)).wait_send(),
                )


def fused(latent, norm_gain, conv_weight, grad_out):
    n = lax.axis_size("tm")
    _, rows_here, columns, channels = latent.shape
    cells = rows_here * columns
    taps, depth = conv_weight.shape[:2]
    line = n // 8
    slots = 2 * (line - 1) + 3
    bf16, f32 = jnp.bfloat16, jnp.float32
    wide = (3, 3, cells + 2 * columns, channels)
    vmem = pl.BlockSpec(memory_space=pltpu.VMEM)
    far = pl.BlockSpec(memory_space=pltpu.HBM)
    refined, grad_latent = pl.pallas_call(
        functools.partial(block_kernel, n, columns),
        out_shape=(
            jax.ShapeDtypeStruct((cells, channels), bf16),
            jax.ShapeDtypeStruct((cells, channels), f32),
        ),
        in_specs=[far] * 4,
        out_specs=(vmem, vmem),
        scratch_shapes=[
            pltpu.VMEM((cells, channels), bf16),
            pltpu.VMEM((1, channels), f32),
            pltpu.VMEM((cells, channels), bf16),
            pltpu.VMEM((taps, line, 2, 2, 2, depth, channels), bf16),
            pltpu.VMEM((3, cells, channels), bf16),
            pltpu.VMEM((2, cells, channels), bf16),
            pltpu.VMEM(wide, bf16),
            pltpu.VMEM(wide, bf16),
            pltpu.VMEM((cells, channels), f32),
            pltpu.VMEM((1, channels), f32),
            pltpu.VMEM((cells, channels), f32),
            pltpu.VMEM((cells, channels), f32),
            pltpu.SemaphoreType.DMA,
            pltpu.SemaphoreType.DMA((3,)),
            pltpu.SemaphoreType.DMA((3, slots)),
            pltpu.SemaphoreType.DMA((taps, slots)),
            pltpu.SemaphoreType.DMA((8,)),
            pltpu.SemaphoreType.DMA((4,)),
        ],
        compiler_params=pltpu.CompilerParams(
            collective_id=0, has_side_effects=True, vmem_limit_bytes=64 * 2**20 - 2**17
        ),
        cost_estimate=pl.CostEstimate(
            flops=4 * taps * cells * channels * channels,
            bytes_accessed=taps * channels * channels * 2,
            transcendentals=2 * cells * channels,
        ),
    )(
        latent.reshape(cells, channels),
        norm_gain.reshape(1, channels),
        conv_weight,
        grad_out.reshape(cells, channels),
    )
    return refined.reshape(latent.shape), grad_latent.reshape(latent.shape)


def shards(latent, norm_gain, conv_weight, grad_out):
    group = latent.shape[3] // GROUPS
    whole_frame = lax.axis_size("rows") == 1 and latent.shape[0] == 1
    if whole_frame and lax.axis_size("tm") % 8 == 0 and group & (group - 1) == 0:
        return fused(latent, norm_gain, conv_weight, grad_out)
    return general(latent, norm_gain, conv_weight, grad_out)


def general(latent, norm_gain, conv_weight, grad_out):
    frames_here, rows_here, columns, channels = latent.shape
    cell_count = lax.axis_size("rows") * rows_here * columns * (channels // GROUPS)
    full_weight = lax.all_gather(conv_weight, "tm", axis=1, tiled=True)
    latent_wide = latent.astype(jnp.float32)
    grouped = grouped_view(latent_wide)
    average = lax.psum(jnp.sum(grouped, axis=(1, 3)), "rows") / cell_count
    centred = grouped - average[:, None, :, None]
    spread = lax.psum(jnp.sum(centred * centred, axis=(1, 3)), "rows") / cell_count
    inverse = lax.rsqrt(spread + epsilon)
    normed_grouped = centred * inverse[:, None, :, None]
    normed = normed_grouped.reshape(latent.shape)
    scaled = normed * norm_gain
    sigmoid_value = jax.nn.sigmoid(scaled)
    activated = (scaled * sigmoid_value).astype(jnp.bfloat16)
    before_one = shifted(activated, "tm", 1)
    before_two = shifted(activated, "tm", 2)
    padded = with_halo(
        jnp.concatenate([before_two, before_one, activated], axis=0), (("rows", 1),), 1
    )
    after_one = shifted(grad_out, "tm", -1)
    after_two = shifted(grad_out, "tm", -2)
    padded_grad = with_halo(
        jnp.concatenate([grad_out, after_one, after_two], axis=0), (("rows", 1),), 1
    )
    padded = widen_columns(padded)
    padded_grad = widen_columns(padded_grad)
    conv_sum = jnp.zeros((frames_here * rows_here * columns, channels), jnp.float32)
    grad_act = jnp.zeros((frames_here * rows_here * columns, channels), jnp.float32)
    for time_tap in range(3):
        for row_tap in range(3):
            for col_tap in range(3):
                tap_weight = full_weight[time_tap * 9 + row_tap * 3 + col_tap]
                window = padded[
                    time_tap : time_tap + frames_here,
                    row_tap : row_tap + rows_here,
                    col_tap : col_tap + columns,
                ]
                conv_sum = conv_sum + jnp.dot(
                    window.reshape(-1, channels), tap_weight, preferred_element_type=jnp.float32
                )
                back_window = padded_grad[
                    2 - time_tap : 2 - time_tap + frames_here,
                    2 - row_tap : 2 - row_tap + rows_here,
                    2 - col_tap : 2 - col_tap + columns,
                ]
                grad_act = grad_act + lax.dot_general(
                    back_window.reshape(-1, channels),
                    tap_weight,
                    (((1,), (1,)), ((), ())),
                    preferred_element_type=jnp.float32,
                )
    refined = (latent_wide + conv_sum.reshape(latent.shape)).astype(jnp.bfloat16)
    grad_scaled = (
        grad_act.reshape(latent.shape) * sigmoid_value * (1.0 + scaled * (1.0 - sigmoid_value))
    )
    grad_normed = grouped_view(grad_scaled * norm_gain)
    first_sum, second_sum = lax.psum(
        (jnp.sum(grad_normed, axis=(1, 3)), jnp.sum(grad_normed * normed_grouped, axis=(1, 3))),
        "rows",
    )
    first = first_sum / cell_count
    second = second_sum / cell_count
    grad_norm_part = (
        grad_normed - first[:, None, :, None] - normed_grouped * second[:, None, :, None]
    ) * inverse[:, None, :, None]
    grad_latent = grad_out.astype(jnp.float32) + grad_norm_part.reshape(latent.shape)
    return (refined, grad_latent)


def solution(mesh):
    placed = (P("tm", "rows", None, None), P(), P(None, "tm", None), P("tm", "rows", None, None))
    return jax.shard_map(
        shards,
        mesh=mesh,
        in_specs=placed,
        out_specs=(P("tm", "rows", None, None), P("tm", "rows", None, None)),
        check_vma=False,
    )
```

```python
import functools

import jax
import jax.numpy as jnp
from jax import lax
from jax.experimental import pallas as pl
from jax.experimental.pallas import tpu as pltpu
from jax.sharding import PartitionSpec as P

GROUPS = 32


epsilon = 1e-06


def shifted(block, axis, distance):
    devices = range(lax.axis_size(axis))
    route = [(i - distance, i) for i in devices if i - distance in devices]
    return lax.ppermute(block, axis, route)


def with_halo(shard, sides, width):
    for axis, dim in sides:
        size, length = (lax.axis_size(axis), shard.shape[dim])
        up = [(i, (i + 1) % size) for i in range(size - 1)]
        down = [(j, i) for i, j in up]
        last = lax.slice_in_dim(shard, length - width, length, axis=dim)
        first = lax.slice_in_dim(shard, 0, width, axis=dim)
        before = lax.ppermute(last, axis, up)
        after = lax.ppermute(first, axis, down)
        shard = jnp.concatenate([before, shard, after], axis=dim)
    return shard


def grouped_view(values):
    return values.reshape(
        values.shape[0], values.shape[1] * values.shape[2], GROUPS, values.shape[3] // GROUPS
    )


def widen_columns(values):
    return jnp.pad(values, ((0, 0), (0, 0), (1, 1), (0, 0)))


def fill_same(same_ref, group):
    shift = group.bit_length() - 1
    shape = same_ref.shape
    left = lax.shift_right_logical(lax.broadcasted_iota(jnp.int32, shape, 0), shift)
    right = lax.shift_right_logical(lax.broadcasted_iota(jnp.int32, shape, 1), shift)
    same_ref[...] = jnp.where(left == right, 1.0, 0.0).astype(jnp.float32)


def group_mean(rows, same_ref, cells):
    return (
        jnp.dot(
            rows,
            same_ref[...],
            preferred_element_type=jnp.float32,
            precision=lax.Precision.HIGHEST,
        )
        / cells
    )


def eight(row):
    return jnp.broadcast_to(row, (8, row.shape[1]))


def sums_of(values):
    return jnp.sum(values, axis=0, keepdims=True)


def block_kernel(
    n,
    columns,
    latent_hbm,
    gain_hbm,
    weight_ref,
    grad_hbm,
    refined_ref,
    out_ref,
    latent_ref,
    gain_ref,
    grad_ref,
    whole,
    act_halo,
    grad_halo,
    act_wide,
    grad_wide,
    normed_ref,
    slope_ref,
    same_ref,
    inverse_ref,
    conv_acc,
    grad_acc,
    own_sem,
    fetch_sem,
    send_sem,
    recv_sem,
    halo_send,
    halo_recv,
):
    me = lax.axis_index("tm")
    depth = n // 8
    core = lax.rem(me, 2)
    px = lax.rem(lax.div(me, 2), 2)
    py = lax.rem(lax.div(me, 4), 2)
    pz = lax.div(me, 8)
    cells, channels = latent_ref.shape
    taps = weight_ref.shape[0]
    group = channels // GROUPS
    neighbour = {
        "x": me + 2 - 4 * px,
        "y": me + 4 - 8 * py,
        "core": me + 1 - 2 * core,
        "up": me + 8,
        "down": me - 8,
    }

    own_copy = pltpu.make_async_copy(weight_ref, whole.at[:, pz, py, px, core], own_sem)
    own_copy.start()
    fetches = [
        pltpu.make_async_copy(source, place, fetch_sem.at[i])
        for i, (source, place) in enumerate(
            ((grad_hbm, grad_ref), (latent_hbm, latent_ref), (gain_hbm, gain_ref))
        )
    ]
    for fetch in fetches:
        fetch.start()

    barrier = pltpu.get_barrier_semaphore()

    def greet(other):
        pl.semaphore_signal(
            barrier, inc=1, device_id={"tm": other}, device_id_type=pl.DeviceIdType.MESH
        )

    for name in ("x", "y", "core"):
        greet(neighbour[name])
    linked = [
        (pz < depth - 1, me + 8),
        (pz > 0, me - 8),
        (me < n - 1, me + 1),
        (me < n - 2, me + 2),
        (me > 0, me - 1),
        (me > 1, me - 2),
    ]
    expected = jnp.int32(3)
    for there, other in linked:
        pl.when(there)(functools.partial(greet, other))
        expected = expected + there.astype(jnp.int32)
    fill_same(same_ref, group)
    conv_acc[...] = jnp.zeros_like(conv_acc)
    grad_acc[...] = jnp.zeros_like(grad_acc)
    own_copy.wait()
    pl.semaphore_wait(barrier, expected)

    n_last_z = (taps + 1) // 4
    n_b = (taps - n_last_z) // 2
    n_c = taps - n_last_z - n_b
    rounds = n_c
    line_first = (*range(depth), depth + 1, depth + 3, depth + 4)
    line_last = (0, 1, *range(2, 2 * depth + 1, 2), 2 * depth + 1)
    kinds = [
        (("z", "x", "y"), 0, n_b, line_first),
        (("z", "y", "x"), n_b, n_c, line_first),
        (("x", "y", "z"), n_b + n_c, n_last_z, line_last),
    ]
    slots = {("up", s): s for s in range(depth - 1)}
    slots.update({("down", s): depth - 1 + s for s in range(depth - 1)})
    for name in ("x", "y", "core"):
        slots[name] = len(slots)

    def item(tap, held, **at):
        parts = [
            at.get(name, slice(None) if name in held else mine)
            for name, mine in (("z", pz), ("y", py), ("x", px), ("core", core))
        ]
        return whole.at[(tap, *parts)]

    def copy(kind, tap, what, target, slot):
        return pltpu.make_async_remote_copy(
            src_ref=what,
            dst_ref=what,
            send_sem=send_sem.at[kind, slots[slot]],
            recv_sem=recv_sem.at[0 if isinstance(tap, pl.Slice) else tap, slots[slot]],
            device_id={"tm": target},
            device_id_type=pl.DeviceIdType.MESH,
        )

    def steps_of(kind, order):
        sends, receives, waits = [], [], []
        held = ()

        def hop(name, held):
            other = {"x": 1 - px, "y": 1 - py, "core": 1 - core}[name]
            sends.append(
                [(None, lambda tap: copy(kind, tap, item(tap, held), neighbour[name], name))]
            )
            receives.append(
                [
                    (
                        None,
                        lambda tap: copy(
                            kind, tap, item(tap, held, **{name: other}), neighbour[name], name
                        ),
                    )
                ]
            )

        def line(step, held):
            def sent(way, sign):
                return lambda tap: copy(
                    kind, tap, item(tap, held, z=pz - sign * step), neighbour[way], (way, step)
                )

            def got(way, sign):
                return lambda tap: copy(
                    kind,
                    tap,
                    item(tap, held, z=pz - sign * (step + 1)),
                    neighbour["down" if way == "up" else "up"],
                    (way, step),
                )

            sends.append(
                [
                    ((pz < depth - 1) & (pz - step >= 0), sent("up", 1)),
                    ((pz > 0) & (pz + step <= depth - 1), sent("down", -1)),
                ]
            )
            receives.append(
                [
                    (pz - step - 1 >= 0, got("up", 1)),
                    (pz + step + 1 <= depth - 1, got("down", -1)),
                ]
            )

        for name in order + ("core",):
            if name == "z":
                for step in range(depth - 1):
                    line(step, held)
            else:
                hop(name, held)
            held = held + (name,)
        return sends, receives

    plans = [steps_of(kind, entry[0]) for kind, entry in enumerate(kinds)]
    stages = len(plans[0][0])

    def guarded(condition, action):
        if condition is None:
            action()
        else:
            pl.when(condition)(action)

    def tap_of(kind, r):
        _, first, count, _ = kinds[kind]
        if count >= rounds - 1:
            return first + r, (r >= 0) & (r < count)
        spread_out = r * count
        return (
            first + lax.div(spread_out, rounds),
            (r >= 0) & (r < rounds) & (lax.rem(spread_out, rounds) < count),
        )

    def advance(tick, low, high):
        for stage in range(high - 1, low - 1, -1):
            for kind in range(len(kinds)):
                tap, valid = tap_of(kind, tick - kinds[kind][3][stage])
                sends, receives = plans[kind]

                @pl.when(valid)
                def _():
                    if stage > 0:
                        for condition, make in receives[stage - 1]:
                            guarded(condition, lambda: make(tap).wait_recv())
                    if stage < stages:
                        for condition, make in sends[stage]:
                            guarded(condition, lambda: make(tap).start())

    def use_tap(tap):
        a = lax.div(tap, 9)
        b = lax.rem(lax.div(tap, 3), 3)
        e = lax.rem(tap, 3)
        inner = cells - columns

        def rows_of(out_first, in_first, count):
            weights = whole[tap].reshape(channels, channels)
            conv_acc[out_first : out_first + count] += jnp.dot(
                act_wide[a, e, columns + in_first : columns + in_first + count],
                weights,
                preferred_element_type=jnp.float32,
            )
            grad_acc[in_first : in_first + count] += lax.dot_general(
                grad_wide[2 - a, 2 - e, columns + out_first : columns + out_first + count],
                weights,
                (((1,), (1,)), ((), ())),
                preferred_element_type=jnp.float32,
            )

        pl.when(b == 0)(lambda: rows_of(columns, 0, inner))
        pl.when(b == 1)(lambda: rows_of(0, 0, cells))
        pl.when(b == 2)(lambda: rows_of(0, columns, inner))

    def compute(tick):
        for kind in range(len(kinds)):
            tap, valid = tap_of(kind, tick - kinds[kind][3][stages])
            pl.when(valid)(functools.partial(use_tap, tap))

    def halo(source, target, place, slot, again=0):
        return pltpu.make_async_remote_copy(
            src_ref=source,
            dst_ref=place,
            send_sem=halo_send.at[slot + again],
            recv_sem=halo_recv.at[slot],
            device_id={"tm": target},
            device_id_type=pl.DeviceIdType.MESH,
        )

    own_act = act_halo.at[2]
    grad_copies = [
        (me > 0, me < n - 1, halo(grad_ref, me - 1, grad_halo.at[0], 0)),
        ((me > 1) & (core == 1), me < n - 2, halo(grad_ref, me - 2, grad_halo.at[1], 1)),
    ]
    act_copies = [
        (me < n - 1, me > 0, halo(own_act, me + 1, act_halo.at[1], 2)),
        ((me < n - 2) & (core == 0), me > 1, halo(own_act, me + 2, act_halo.at[0], 3)),
    ]
    passed_on = [
        ((me < n - 2) & (core == 1), halo(grad_halo.at[0], me - 1, grad_halo.at[1], 1, 4)),
        ((me > 1) & (core == 0), halo(act_halo.at[1], me + 1, act_halo.at[0], 3, 4)),
    ]

    advance(0, 0, 1)
    for fetch in fetches:
        fetch.wait()
    for sends_it, _, this in grad_copies:
        pl.when(sends_it)(this.start)

    latent_wide = latent_ref[...].astype(jnp.float32)
    gain = gain_ref[...]
    count = cells * group
    average = group_mean(eight(sums_of(latent_wide)), same_ref, count)[0:1]
    centred = latent_wide - average
    spread = group_mean(eight(sums_of(centred * centred)), same_ref, count)[0:1]
    inverse = lax.rsqrt(spread + epsilon)
    inverse_ref[...] = inverse
    normed = centred * inverse
    normed_ref[...] = normed
    scaled = normed * gain
    sigmoid_value = jax.nn.sigmoid(scaled)
    activated = scaled * sigmoid_value
    own_act[...] = activated.astype(jnp.bfloat16)
    for sends_it, _, this in act_copies:
        pl.when(sends_it)(this.start)
    column = lax.rem(lax.broadcasted_iota(jnp.int32, (cells, channels), 0), columns)
    edge = jnp.zeros((columns, channels), jnp.bfloat16)

    def widen(frame, wide, place):
        values = frame.astype(jnp.float32)
        left = jnp.where(column == 0, 0.0, pltpu.roll(values, 1, 0))
        right = jnp.where(column == columns - 1, 0.0, pltpu.roll(values, cells - 1, 0))
        for e, part in enumerate((left, values, right)):
            wide[place, e, 0:columns] = edge
            wide[place, e, columns : columns + cells] = part.astype(jnp.bfloat16)
            wide[place, e, columns + cells : 2 * columns + cells] = edge

    def keep_slope():
        scaled = normed_ref[...] * gain_ref[...]
        sigmoid_value = jax.nn.sigmoid(scaled)
        slope_ref[...] = (
            sigmoid_value * (1.0 + scaled * (1.0 - sigmoid_value)) * gain_ref[...]
        )

    def take(copies, d, buffer, at, wide, place):
        _, gets_it, this = copies[d]
        pl.when(gets_it)(this.wait_recv)
        if d == 0:
            passes, onward = passed_on[copies is act_copies]
            pl.when(passes)(onward.start)

        @pl.when(jnp.logical_not(gets_it))
        def _():
            buffer[at] = jnp.zeros((cells, channels), jnp.bfloat16)

        widen(buffer[at], wide, place)

    jobs = [
        keep_slope,
        lambda: widen(act_halo[2], act_wide, 2),
        lambda: widen(grad_ref[...], grad_wide, 0),
        lambda: take(grad_copies, 0, grad_halo, 0, grad_wide, 1),
        lambda: take(act_copies, 0, act_halo, 1, act_wide, 1),
        lambda: take(grad_copies, 1, grad_halo, 1, grad_wide, 2),
        lambda: take(act_copies, 1, act_halo, 0, act_wide, 0),
    ]

    def early(tick, carry):
        advance(tick, 0, stages)
        for i, job in enumerate(jobs):
            pl.when(tick == 1 + i)(job)
        return carry

    first_use = min(entry[3][stages] for entry in kinds)
    last_use = max(entry[3][stages] for entry in kinds)
    lax.fori_loop(1, first_use, early, 0)

    def late(tick, carry):
        advance(tick, 0, stages + 1)
        compute(tick)
        return carry

    lax.fori_loop(first_use, rounds + last_use, late, 0)

    refined_ref[...] = (latent_ref[...].astype(jnp.float32) + conv_acc[...]).astype(jnp.bfloat16)
    normed = normed_ref[...]
    grad_normed = grad_acc[...] * slope_ref[...]
    upper = lax.broadcasted_iota(jnp.int32, (8, channels), 0) < 4
    means = group_mean(
        jnp.where(upper, eight(sums_of(grad_normed)), eight(sums_of(grad_normed * normed))),
        same_ref,
        count,
    )
    first, second = means[0:1], means[4:5]
    out_ref[...] = grad_ref[...].astype(jnp.float32) + (
        grad_normed - first - normed * second
    ) * inverse_ref[...]

    for sends_it, _, this in grad_copies + act_copies:
        pl.when(sends_it)(this.wait_send)
    for passes, onward in passed_on:
        pl.when(passes)(onward.wait_send)
    for kind, (order, first_tap, count_taps, _) in enumerate(kinds):
        for stage in plans[kind][0]:
            for condition, make in stage:
                guarded(
                    condition,
                    lambda: make(pl.ds(first_tap, count_taps)).wait_send(),
                )


def fused(latent, norm_gain, conv_weight, grad_out):
    n = lax.axis_size("tm")
    _, rows_here, columns, channels = latent.shape
    cells = rows_here * columns
    taps, depth = conv_weight.shape[:2]
    line = n // 8
    slots = 2 * (line - 1) + 3
    bf16, f32 = jnp.bfloat16, jnp.float32
    wide = (3, 3, cells + 2 * columns, channels)
    vmem = pl.BlockSpec(memory_space=pltpu.VMEM)
    far = pl.BlockSpec(memory_space=pltpu.HBM)
    refined, grad_latent = pl.pallas_call(
        functools.partial(block_kernel, n, columns),
        out_shape=(
            jax.ShapeDtypeStruct((cells, channels), bf16),
            jax.ShapeDtypeStruct((cells, channels), f32),
        ),
        in_specs=[far] * 4,
        out_specs=(vmem, vmem),
        scratch_shapes=[
            pltpu.VMEM((cells, channels), bf16),
            pltpu.VMEM((1, channels), f32),
            pltpu.VMEM((cells, channels), bf16),
            pltpu.VMEM((taps, line, 2, 2, 2, depth, channels), bf16),
            pltpu.VMEM((3, cells, channels), bf16),
            pltpu.VMEM((2, cells, channels), bf16),
            pltpu.VMEM(wide, bf16),
            pltpu.VMEM(wide, bf16),
            pltpu.VMEM((cells, channels), f32),
            pltpu.VMEM((cells, channels), f32),
            pltpu.VMEM((channels, channels), f32),
            pltpu.VMEM((1, channels), f32),
            pltpu.VMEM((cells, channels), f32),
            pltpu.VMEM((cells, channels), f32),
            pltpu.SemaphoreType.DMA,
            pltpu.SemaphoreType.DMA((3,)),
            pltpu.SemaphoreType.DMA((3, slots)),
            pltpu.SemaphoreType.DMA((taps, slots)),
            pltpu.SemaphoreType.DMA((8,)),
            pltpu.SemaphoreType.DMA((4,)),
        ],
        compiler_params=pltpu.CompilerParams(
            collective_id=0, has_side_effects=True, vmem_limit_bytes=64 * 2**20 - 2**17
        ),
        cost_estimate=pl.CostEstimate(
            flops=4 * taps * cells * channels * channels,
            bytes_accessed=taps * channels * channels * 2,
            transcendentals=2 * cells * channels,
        ),
    )(
        latent.reshape(cells, channels),
        norm_gain.reshape(1, channels),
        conv_weight,
        grad_out.reshape(cells, channels),
    )
    return refined.reshape(latent.shape), grad_latent.reshape(latent.shape)


def shards(latent, norm_gain, conv_weight, grad_out):
    group = latent.shape[3] // GROUPS
    whole_frame = lax.axis_size("rows") == 1 and latent.shape[0] == 1
    if whole_frame and lax.axis_size("tm") % 8 == 0 and group & (group - 1) == 0:
        return fused(latent, norm_gain, conv_weight, grad_out)
    return general(latent, norm_gain, conv_weight, grad_out)


def general(latent, norm_gain, conv_weight, grad_out):
    frames_here, rows_here, columns, channels = latent.shape
    cell_count = lax.axis_size("rows") * rows_here * columns * (channels // GROUPS)
    full_weight = lax.all_gather(conv_weight, "tm", axis=1, tiled=True)
    latent_wide = latent.astype(jnp.float32)
    grouped = grouped_view(latent_wide)
    average = lax.psum(jnp.sum(grouped, axis=(1, 3)), "rows") / cell_count
    centred = grouped - average[:, None, :, None]
    spread = lax.psum(jnp.sum(centred * centred, axis=(1, 3)), "rows") / cell_count
    inverse = lax.rsqrt(spread + epsilon)
    normed_grouped = centred * inverse[:, None, :, None]
    normed = normed_grouped.reshape(latent.shape)
    scaled = normed * norm_gain
    sigmoid_value = jax.nn.sigmoid(scaled)
    activated = (scaled * sigmoid_value).astype(jnp.bfloat16)
    before_one = shifted(activated, "tm", 1)
    before_two = shifted(activated, "tm", 2)
    padded = with_halo(
        jnp.concatenate([before_two, before_one, activated], axis=0), (("rows", 1),), 1
    )
    after_one = shifted(grad_out, "tm", -1)
    after_two = shifted(grad_out, "tm", -2)
    padded_grad = with_halo(
        jnp.concatenate([grad_out, after_one, after_two], axis=0), (("rows", 1),), 1
    )
    padded = widen_columns(padded)
    padded_grad = widen_columns(padded_grad)
    conv_sum = jnp.zeros((frames_here * rows_here * columns, channels), jnp.float32)
    grad_act = jnp.zeros((frames_here * rows_here * columns, channels), jnp.float32)
    for time_tap in range(3):
        for row_tap in range(3):
            for col_tap in range(3):
                tap_weight = full_weight[time_tap * 9 + row_tap * 3 + col_tap]
                window = padded[
                    time_tap : time_tap + frames_here,
                    row_tap : row_tap + rows_here,
                    col_tap : col_tap + columns,
                ]
                conv_sum = conv_sum + jnp.dot(
                    window.reshape(-1, channels), tap_weight, preferred_element_type=jnp.float32
                )
                back_window = padded_grad[
                    2 - time_tap : 2 - time_tap + frames_here,
                    2 - row_tap : 2 - row_tap + rows_here,
                    2 - col_tap : 2 - col_tap + columns,
                ]
                grad_act = grad_act + lax.dot_general(
                    back_window.reshape(-1, channels),
                    tap_weight,
                    (((1,), (1,)), ((), ())),
                    preferred_element_type=jnp.float32,
                )
    refined = (latent_wide + conv_sum.reshape(latent.shape)).astype(jnp.bfloat16)
    grad_scaled = (
        grad_act.reshape(latent.shape) * sigmoid_value * (1.0 + scaled * (1.0 - sigmoid_value))
    )
    grad_normed = grouped_view(grad_scaled * norm_gain)
    first_sum, second_sum = lax.psum(
        (jnp.sum(grad_normed, axis=(1, 3)), jnp.sum(grad_normed * normed_grouped, axis=(1, 3))),
        "rows",
    )
    first = first_sum / cell_count
    second = second_sum / cell_count
    grad_norm_part = (
        grad_normed - first[:, None, :, None] - normed_grouped * second[:, None, :, None]
    ) * inverse[:, None, :, None]
    grad_latent = grad_out.astype(jnp.float32) + grad_norm_part.reshape(latent.shape)
    return (refined, grad_latent)


def solution(mesh):
    placed = (P("tm", "rows", None, None), P(), P(None, "tm", None), P("tm", "rows", None, None))
    return jax.shard_map(
        shards,
        mesh=mesh,
        in_specs=placed,
        out_specs=(P("tm", "rows", None, None), P("tm", "rows", None, None)),
        check_vma=False,
    )
```

```python
import functools

import jax
import jax.numpy as jnp
from jax import lax
from jax.experimental import pallas as pl
from jax.experimental.pallas import tpu as pltpu
from jax.sharding import PartitionSpec as P

GROUPS = 32


epsilon = 1e-06


def shifted(block, axis, distance):
    devices = range(lax.axis_size(axis))
    route = [(i - distance, i) for i in devices if i - distance in devices]
    return lax.ppermute(block, axis, route)


def with_halo(shard, sides, width):
    for axis, dim in sides:
        size, length = (lax.axis_size(axis), shard.shape[dim])
        up = [(i, (i + 1) % size) for i in range(size - 1)]
        down = [(j, i) for i, j in up]
        last = lax.slice_in_dim(shard, length - width, length, axis=dim)
        first = lax.slice_in_dim(shard, 0, width, axis=dim)
        before = lax.ppermute(last, axis, up)
        after = lax.ppermute(first, axis, down)
        shard = jnp.concatenate([before, shard, after], axis=dim)
    return shard


def grouped_view(values):
    return values.reshape(
        values.shape[0], values.shape[1] * values.shape[2], GROUPS, values.shape[3] // GROUPS
    )


def widen_columns(values):
    return jnp.pad(values, ((0, 0), (0, 0), (1, 1), (0, 0)))


def fill_same(same_ref, group):
    shift = group.bit_length() - 1
    shape = same_ref.shape
    left = lax.shift_right_logical(lax.broadcasted_iota(jnp.int32, shape, 0), shift)
    right = lax.shift_right_logical(lax.broadcasted_iota(jnp.int32, shape, 1), shift)
    same_ref[...] = jnp.where(left == right, 1.0, 0.0).astype(jnp.float32)


def group_mean(rows, same_ref, cells):
    return (
        jnp.dot(
            rows,
            same_ref[...],
            preferred_element_type=jnp.float32,
            precision=lax.Precision.HIGHEST,
        )
        / cells
    )


def eight(row):
    return jnp.broadcast_to(row, (8, row.shape[1]))


def sums_of(values):
    return jnp.sum(values, axis=0, keepdims=True)


def block_kernel(
    n,
    columns,
    latent_hbm,
    gain_hbm,
    weight_ref,
    grad_hbm,
    refined_ref,
    out_ref,
    latent_ref,
    gain_ref,
    grad_ref,
    whole,
    act_halo,
    grad_halo,
    act_wide,
    grad_wide,
    normed_ref,
    slope_ref,
    same_ref,
    inverse_ref,
    conv_acc,
    grad_acc,
    own_sem,
    fetch_sem,
    send_sem,
    recv_sem,
    halo_send,
    halo_recv,
):
    me = lax.axis_index("tm")
    depth = n // 8
    core = lax.rem(me, 2)
    px = lax.rem(lax.div(me, 2), 2)
    py = lax.rem(lax.div(me, 4), 2)
    pz = lax.div(me, 8)
    cells, channels = latent_ref.shape
    taps = weight_ref.shape[0]
    group = channels // GROUPS
    neighbour = {
        "x": me + 2 - 4 * px,
        "y": me + 4 - 8 * py,
        "core": me + 1 - 2 * core,
        "up": me + 8,
        "down": me - 8,
    }

    own_copy = pltpu.make_async_copy(weight_ref, whole.at[:, pz, py, px, core], own_sem)
    own_copy.start()
    fetches = [
        pltpu.make_async_copy(source, place, fetch_sem.at[i])
        for i, (source, place) in enumerate(
            ((grad_hbm, grad_ref), (latent_hbm, latent_ref), (gain_hbm, gain_ref))
        )
    ]
    for fetch in fetches:
        fetch.start()

    barrier = pltpu.get_barrier_semaphore()

    def greet(other):
        pl.semaphore_signal(
            barrier, inc=1, device_id={"tm": other}, device_id_type=pl.DeviceIdType.MESH
        )

    for name in ("x", "y", "core"):
        greet(neighbour[name])
    linked = [
        (pz < depth - 1, me + 8),
        (pz > 0, me - 8),
        (me < n - 1, me + 1),
        (me < n - 2, me + 2),
        (me > 0, me - 1),
        (me > 1, me - 2),
    ]
    expected = jnp.int32(3)
    for there, other in linked:
        pl.when(there)(functools.partial(greet, other))
        expected = expected + there.astype(jnp.int32)
    fill_same(same_ref, group)
    conv_acc[...] = jnp.zeros_like(conv_acc)
    grad_acc[...] = jnp.zeros_like(grad_acc)
    own_copy.wait()
    pl.semaphore_wait(barrier, expected)

    n_last_z = (taps + 1) // 4
    n_b = (taps - n_last_z) // 2
    n_c = taps - n_last_z - n_b
    rounds = n_c
    ahead = 3
    later = max(0, 4 - depth)
    line_first = (-ahead, *range(depth - 1), depth, depth + 2, depth + 3 + later)
    line_last = (-ahead, 0, *range(1, 2 * depth, 2), 2 * depth + later)
    kinds = [
        (("z", "x", "y"), 0, n_b, line_first),
        (("z", "y", "x"), n_b, n_c, line_first),
        (("x", "y", "z"), n_b + n_c, n_last_z, line_last),
    ]
    slots = {("up", s): s for s in range(depth - 1)}
    slots.update({("down", s): depth - 1 + s for s in range(depth - 1)})
    for name in ("x", "y", "core"):
        slots[name] = len(slots)

    def item(tap, held, **at):
        parts = [
            at.get(name, slice(None) if name in held else mine)
            for name, mine in (("z", pz), ("y", py), ("x", px), ("core", core))
        ]
        return whole.at[(tap, *parts)]

    def copy(kind, tap, what, target, slot):
        return pltpu.make_async_remote_copy(
            src_ref=what,
            dst_ref=what,
            send_sem=send_sem.at[kind, slots[slot]],
            recv_sem=recv_sem.at[0 if isinstance(tap, pl.Slice) else tap, slots[slot]],
            device_id={"tm": target},
            device_id_type=pl.DeviceIdType.MESH,
        )

    def steps_of(kind, order):
        sends, receives, waits = [], [], []
        held = ()

        def hop(name, held):
            other = {"x": 1 - px, "y": 1 - py, "core": 1 - core}[name]
            sends.append(
                [(None, lambda tap: copy(kind, tap, item(tap, held), neighbour[name], name))]
            )
            receives.append(
                [
                    (
                        None,
                        lambda tap: copy(
                            kind, tap, item(tap, held, **{name: other}), neighbour[name], name
                        ),
                    )
                ]
            )

        def line(step, held):
            def sent(way, sign):
                return lambda tap: copy(
                    kind, tap, item(tap, held, z=pz - sign * step), neighbour[way], (way, step)
                )

            def got(way, sign):
                return lambda tap: copy(
                    kind,
                    tap,
                    item(tap, held, z=pz - sign * (step + 1)),
                    neighbour["down" if way == "up" else "up"],
                    (way, step),
                )

            sends.append(
                [
                    ((pz < depth - 1) & (pz - step >= 0), sent("up", 1)),
                    ((pz > 0) & (pz + step <= depth - 1), sent("down", -1)),
                ]
            )
            receives.append(
                [
                    (pz - step - 1 >= 0, got("up", 1)),
                    (pz + step + 1 <= depth - 1, got("down", -1)),
                ]
            )

        for name in order + ("core",):
            if name == "z":
                for step in range(depth - 1):
                    line(step, held)
            else:
                hop(name, held)
            held = held + (name,)
        return sends, receives

    plans = [steps_of(kind, entry[0]) for kind, entry in enumerate(kinds)]
    stages = len(plans[0][0])

    def guarded(condition, action):
        if condition is None:
            action()
        else:
            pl.when(condition)(action)

    def tap_of(kind, r):
        _, first, count, _ = kinds[kind]
        if count >= rounds - 1:
            return first + r, (r >= 0) & (r < count)
        spread_out = r * count
        return (
            first + lax.div(spread_out, rounds),
            (r >= 0) & (r < rounds) & (lax.rem(spread_out, rounds) < count),
        )

    def advance(tick, low, high):
        for stage in range(high - 1, low - 1, -1):
            for kind in range(len(kinds)):
                tap, valid = tap_of(kind, tick - kinds[kind][3][stage])
                sends, receives = plans[kind]

                @pl.when(valid)
                def _():
                    if stage > 0:
                        for condition, make in receives[stage - 1]:
                            guarded(condition, lambda: make(tap).wait_recv())
                    if stage < stages:
                        for condition, make in sends[stage]:
                            guarded(condition, lambda: make(tap).start())

    def use_tap(tap):
        a = lax.div(tap, 9)
        b = lax.rem(lax.div(tap, 3), 3)
        e = lax.rem(tap, 3)
        weights = whole[tap].reshape(channels, channels)
        forward = act_wide[a, e, pl.ds(pl.multiple_of(b * columns, columns), cells)]
        conv_acc[...] += jnp.dot(forward, weights, preferred_element_type=jnp.float32)
        back = grad_wide[
            2 - a, 2 - e, pl.ds(pl.multiple_of((2 - b) * columns, columns), cells)
        ]
        grad_acc[...] += lax.dot_general(
            back, weights, (((1,), (1,)), ((), ())), preferred_element_type=jnp.float32
        )

    def compute(tick):
        for kind in range(len(kinds)):
            tap, valid = tap_of(kind, tick - kinds[kind][3][stages])
            pl.when(valid)(functools.partial(use_tap, tap))

    def halo(source, target, place, slot, again=0):
        return pltpu.make_async_remote_copy(
            src_ref=source,
            dst_ref=place,
            send_sem=halo_send.at[slot + again],
            recv_sem=halo_recv.at[slot],
            device_id={"tm": target},
            device_id_type=pl.DeviceIdType.MESH,
        )

    own_act = act_halo.at[2]
    grad_copies = [
        (me > 0, me < n - 1, halo(grad_ref, me - 1, grad_halo.at[0], 0)),
        ((me > 1) & (core == 1), me < n - 2, halo(grad_ref, me - 2, grad_halo.at[1], 1)),
    ]
    act_copies = [
        (me < n - 1, me > 0, halo(own_act, me + 1, act_halo.at[1], 2)),
        ((me < n - 2) & (core == 0), me > 1, halo(own_act, me + 2, act_halo.at[0], 3)),
    ]
    passed_on = [
        ((me < n - 2) & (core == 1), halo(grad_halo.at[0], me - 1, grad_halo.at[1], 1, 4)),
        ((me > 1) & (core == 0), halo(act_halo.at[1], me + 1, act_halo.at[0], 3, 4)),
    ]

    for tick in range(-ahead, 0):
        advance(tick, 0, 1)
    fetches[0].wait()
    for sends_it, _, this in grad_copies:
        pl.when(sends_it)(this.start)

    count = cells * group

    def normalise():
        for fetch in fetches[1:]:
            fetch.wait()
        latent_wide = latent_ref[...].astype(jnp.float32)
        gain = gain_ref[...]
        average = group_mean(eight(sums_of(latent_wide)), same_ref, count)[0:1]
        centred = latent_wide - average
        spread = group_mean(eight(sums_of(centred * centred)), same_ref, count)[0:1]
        inverse = lax.rsqrt(spread + epsilon)
        inverse_ref[...] = inverse
        normed = centred * inverse
        normed_ref[...] = normed
        scaled = normed * gain
        sigmoid_value = jax.nn.sigmoid(scaled)
        slope_ref[...] = sigmoid_value * (1.0 + scaled * (1.0 - sigmoid_value)) * gain
        own_act[...] = (scaled * sigmoid_value).astype(jnp.bfloat16)
        for sends_it, _, this in act_copies:
            pl.when(sends_it)(this.start)

    def widen_own():
        widen(act_halo[2], act_wide, 2)
        widen(grad_ref[...], grad_wide, 0)

    column = lax.rem(lax.broadcasted_iota(jnp.int32, (cells, channels), 0), columns)
    edge = jnp.zeros((columns, channels), jnp.bfloat16)

    def widen(frame, wide, place):
        values = frame.astype(jnp.float32)
        left = jnp.where(column == 0, 0.0, pltpu.roll(values, 1, 0))
        right = jnp.where(column == columns - 1, 0.0, pltpu.roll(values, cells - 1, 0))
        for e, part in enumerate((left, values, right)):
            wide[place, e, 0:columns] = edge
            wide[place, e, columns : columns + cells] = part.astype(jnp.bfloat16)
            wide[place, e, columns + cells : 2 * columns + cells] = edge

    def take(copies, d, buffer, at, wide, place):
        _, gets_it, this = copies[d]
        pl.when(gets_it)(this.wait_recv)
        if d == 0:
            passes, onward = passed_on[copies is act_copies]
            pl.when(passes)(onward.start)

        @pl.when(jnp.logical_not(gets_it))
        def _():
            buffer[at] = jnp.zeros((cells, channels), jnp.bfloat16)

        widen(buffer[at], wide, place)

    jobs = [
        normalise,
        widen_own,
        lambda: take(grad_copies, 0, grad_halo, 0, grad_wide, 1),
        lambda: take(act_copies, 0, act_halo, 1, act_wide, 1),
        lambda: take(grad_copies, 1, grad_halo, 1, grad_wide, 2),
        lambda: take(act_copies, 1, act_halo, 0, act_wide, 0),
    ]

    def early(tick, carry):
        advance(tick, 0, stages)
        for i, job in enumerate(jobs):
            pl.when(tick == 1 + i)(job)
        return carry

    first_use = min(entry[3][stages] for entry in kinds)
    last_use = max(entry[3][stages] for entry in kinds)
    lax.fori_loop(0, first_use, early, 0)

    def late(tick, carry):
        advance(tick, 0, stages + 1)
        compute(tick)
        return carry

    lax.fori_loop(first_use, rounds + last_use, late, 0)

    refined_ref[...] = (latent_ref[...].astype(jnp.float32) + conv_acc[...]).astype(jnp.bfloat16)
    normed = normed_ref[...]
    grad_normed = grad_acc[...] * slope_ref[...]
    upper = lax.broadcasted_iota(jnp.int32, (8, channels), 0) < 4
    means = group_mean(
        jnp.where(upper, eight(sums_of(grad_normed)), eight(sums_of(grad_normed * normed))),
        same_ref,
        count,
    )
    first, second = means[0:1], means[4:5]
    out_ref[...] = grad_ref[...].astype(jnp.float32) + (
        grad_normed - first - normed * second
    ) * inverse_ref[...]

    for sends_it, _, this in grad_copies + act_copies:
        pl.when(sends_it)(this.wait_send)
    for passes, onward in passed_on:
        pl.when(passes)(onward.wait_send)
    for kind, (order, first_tap, count_taps, _) in enumerate(kinds):
        for stage in plans[kind][0]:
            for condition, make in stage:
                guarded(
                    condition,
                    lambda: make(pl.ds(first_tap, count_taps)).wait_send(),
                )


def fused(latent, norm_gain, conv_weight, grad_out):
    n = lax.axis_size("tm")
    _, rows_here, columns, channels = latent.shape
    cells = rows_here * columns
    taps, depth = conv_weight.shape[:2]
    line = n // 8
    slots = 2 * (line - 1) + 3
    bf16, f32 = jnp.bfloat16, jnp.float32
    wide = (3, 3, cells + 2 * columns, channels)
    vmem = pl.BlockSpec(memory_space=pltpu.VMEM)
    far = pl.BlockSpec(memory_space=pltpu.HBM)
    refined, grad_latent = pl.pallas_call(
        functools.partial(block_kernel, n, columns),
        out_shape=(
            jax.ShapeDtypeStruct((cells, channels), bf16),
            jax.ShapeDtypeStruct((cells, channels), f32),
        ),
        in_specs=[far] * 4,
        out_specs=(vmem, vmem),
        scratch_shapes=[
            pltpu.VMEM((cells, channels), bf16),
            pltpu.VMEM((1, channels), f32),
            pltpu.VMEM((cells, channels), bf16),
            pltpu.VMEM((taps, line, 2, 2, 2, depth, channels), bf16),
            pltpu.VMEM((3, cells, channels), bf16),
            pltpu.VMEM((2, cells, channels), bf16),
            pltpu.VMEM(wide, bf16),
            pltpu.VMEM(wide, bf16),
            pltpu.VMEM((cells, channels), f32),
            pltpu.VMEM((cells, channels), f32),
            pltpu.VMEM((channels, channels), f32),
            pltpu.VMEM((1, channels), f32),
            pltpu.VMEM((cells, channels), f32),
            pltpu.VMEM((cells, channels), f32),
            pltpu.SemaphoreType.DMA,
            pltpu.SemaphoreType.DMA((3,)),
            pltpu.SemaphoreType.DMA((3, slots)),
            pltpu.SemaphoreType.DMA((taps, slots)),
            pltpu.SemaphoreType.DMA((8,)),
            pltpu.SemaphoreType.DMA((4,)),
        ],
        compiler_params=pltpu.CompilerParams(
            collective_id=0, has_side_effects=True, vmem_limit_bytes=64 * 2**20 - 2**17
        ),
        cost_estimate=pl.CostEstimate(
            flops=4 * taps * cells * channels * channels,
            bytes_accessed=taps * channels * channels * 2,
            transcendentals=2 * cells * channels,
        ),
    )(
        latent.reshape(cells, channels),
        norm_gain.reshape(1, channels),
        conv_weight,
        grad_out.reshape(cells, channels),
    )
    return refined.reshape(latent.shape), grad_latent.reshape(latent.shape)


def shards(latent, norm_gain, conv_weight, grad_out):
    group = latent.shape[3] // GROUPS
    whole_frame = lax.axis_size("rows") == 1 and latent.shape[0] == 1
    if whole_frame and lax.axis_size("tm") % 8 == 0 and group & (group - 1) == 0:
        return fused(latent, norm_gain, conv_weight, grad_out)
    return general(latent, norm_gain, conv_weight, grad_out)


def general(latent, norm_gain, conv_weight, grad_out):
    frames_here, rows_here, columns, channels = latent.shape
    cell_count = lax.axis_size("rows") * rows_here * columns * (channels // GROUPS)
    full_weight = lax.all_gather(conv_weight, "tm", axis=1, tiled=True)
    latent_wide = latent.astype(jnp.float32)
    grouped = grouped_view(latent_wide)
    average = lax.psum(jnp.sum(grouped, axis=(1, 3)), "rows") / cell_count
    centred = grouped - average[:, None, :, None]
    spread = lax.psum(jnp.sum(centred * centred, axis=(1, 3)), "rows") / cell_count
    inverse = lax.rsqrt(spread + epsilon)
    normed_grouped = centred * inverse[:, None, :, None]
    normed = normed_grouped.reshape(latent.shape)
    scaled = normed * norm_gain
    sigmoid_value = jax.nn.sigmoid(scaled)
    activated = (scaled * sigmoid_value).astype(jnp.bfloat16)
    before_one = shifted(activated, "tm", 1)
    before_two = shifted(activated, "tm", 2)
    padded = with_halo(
        jnp.concatenate([before_two, before_one, activated], axis=0), (("rows", 1),), 1
    )
    after_one = shifted(grad_out, "tm", -1)
    after_two = shifted(grad_out, "tm", -2)
    padded_grad = with_halo(
        jnp.concatenate([grad_out, after_one, after_two], axis=0), (("rows", 1),), 1
    )
    padded = widen_columns(padded)
    padded_grad = widen_columns(padded_grad)
    conv_sum = jnp.zeros((frames_here * rows_here * columns, channels), jnp.float32)
    grad_act = jnp.zeros((frames_here * rows_here * columns, channels), jnp.float32)
    for time_tap in range(3):
        for row_tap in range(3):
            for col_tap in range(3):
                tap_weight = full_weight[time_tap * 9 + row_tap * 3 + col_tap]
                window = padded[
                    time_tap : time_tap + frames_here,
                    row_tap : row_tap + rows_here,
                    col_tap : col_tap + columns,
                ]
                conv_sum = conv_sum + jnp.dot(
                    window.reshape(-1, channels), tap_weight, preferred_element_type=jnp.float32
                )
                back_window = padded_grad[
                    2 - time_tap : 2 - time_tap + frames_here,
                    2 - row_tap : 2 - row_tap + rows_here,
                    2 - col_tap : 2 - col_tap + columns,
                ]
                grad_act = grad_act + lax.dot_general(
                    back_window.reshape(-1, channels),
                    tap_weight,
                    (((1,), (1,)), ((), ())),
                    preferred_element_type=jnp.float32,
                )
    refined = (latent_wide + conv_sum.reshape(latent.shape)).astype(jnp.bfloat16)
    grad_scaled = (
        grad_act.reshape(latent.shape) * sigmoid_value * (1.0 + scaled * (1.0 - sigmoid_value))
    )
    grad_normed = grouped_view(grad_scaled * norm_gain)
    first_sum, second_sum = lax.psum(
        (jnp.sum(grad_normed, axis=(1, 3)), jnp.sum(grad_normed * normed_grouped, axis=(1, 3))),
        "rows",
    )
    first = first_sum / cell_count
    second = second_sum / cell_count
    grad_norm_part = (
        grad_normed - first[:, None, :, None] - normed_grouped * second[:, None, :, None]
    ) * inverse[:, None, :, None]
    grad_latent = grad_out.astype(jnp.float32) + grad_norm_part.reshape(latent.shape)
    return (refined, grad_latent)


def solution(mesh):
    placed = (P("tm", "rows", None, None), P(), P(None, "tm", None), P("tm", "rows", None, None))
    return jax.shard_map(
        shards,
        mesh=mesh,
        in_specs=placed,
        out_specs=(P("tm", "rows", None, None), P("tm", "rows", None, None)),
        check_vma=False,
    )
```
